32 devices in a mesh: leaf: 8 (over z, x), sub: 4 (over y, core).
Axes of the slice: x: 2, y: 2, z: 4, core: 2. Of those that a mesh axis runs over, the one named last changes fastest.
Arguments:
- leaf_right: bfloat16 [128, 512, 256], P(('leaf', 'sub')), may hold values from -6 to 6
- leaf_inverse: bfloat16 [128, 512, 512], P(('leaf', 'sub')), may hold values from -2.5 to 2.5, as said below
- panels: bfloat16 [128, 256, 512], P(('leaf', 'sub')), may hold values from -0.125 to 0.125
- leaf_subtree: int32 [128], P(('leaf', 'sub')), may hold values from 0 to 7, as said below
- panel_block: int32 [128, 4], P(('leaf', 'sub')), may hold values from 0 to 63
- separator_right: bfloat16 [32768, 256], P(('leaf', 'sub')), may hold values from -6 to 6
- separator_inverse: bfloat16 [32768, 512], P(('leaf', 'sub')), may hold values from -2.5 to 2.5, as said below
- separator_factor: bfloat16 [32768, 4096], P(('leaf', 'sub')), may hold values from -1 to 1, as said below
Outputs:
- leaf_solution: bfloat16 [128, 512, 256], P(('leaf', 'sub'))
- separator_solution: bfloat16 [32768, 256], P(('leaf', 'sub'))
The draws below stay inside these ranges and needn't reach their ends.
Inputs may be any that keep to these rules, and one draw needn't show every extreme that they name: `leaf_subtree`: every leaf supernode held by section s of the leaf axis belongs to a subtree between s - (2) and s. Each device of section s holds, for every d from 0 to min(2, s), at least one leaf supernode of subtree s - d. `leaf_inverse`: each 512 x 512 block is lower triangular, with its diagonal between 0.6 and 1.4. `separator_inverse`: each 512 x 512 block is lower triangular, with its diagonal between 0.6 and 1.4. `separator_factor`: within each subtree's 4096 rows, the block of row block q and column block p (blocks of 512) is zero unless q > p.
All inputs are finite; a program needn't handle non-finite values.
Results may differ from the reference program's by a relative error of at most 0.024.
Values may be sent and summed in bfloat16 or wider, within the bound.
A program may use at most 128 MiB of HBM per device.

```python
import math
import jax
import jax.numpy as jnp
from jax import lax

W = 512
WSN = 512
SA = 4096
R = 256
BLK = 64
KB = 4
SPAN = 3
SN_DEV = 4
LEAVES = 128
NSEP = 8
NBS = 64


def triangle(key, count_blocks, width):
    rows = jnp.arange(width)
    lower = (rows[None, :] < rows[:, None]).astype(jnp.float32)
    identity_mask = (rows[None, :] == rows[:, None]).astype(jnp.float32)
    noise_key, diagonal_key = jax.random.split(key)
    noise = jnp.clip(jax.random.normal(noise_key, (count_blocks, width, width), jnp.float32), -4.0, 4.0)
    spread = 0.6 / jnp.sqrt(rows.astype(jnp.float32) + 1.0)
    diagonal = jax.random.uniform(diagonal_key, (count_blocks, width), jnp.float32, 0.6, 1.4)
    return noise * lower[None, :, :] * spread[None, :, None] + diagonal[:, :, None] * identity_mask[None, :, :]


def draw_leaf_inverse(key, part):
    return triangle(key, LEAVES, W).astype(jnp.bfloat16)


def draw_separator_inverse(key, part):
    return triangle(key, NSEP * (SA // WSN), WSN).reshape(NSEP * SA, WSN).astype(jnp.bfloat16)


def draw_separator_factor(key, part):
    rows = jnp.arange(SA)
    blocks = rows // WSN
    next_block = (blocks[:, None] == blocks[None, :] + 1).astype(jnp.float32)
    far_block = (blocks[:, None] > blocks[None, :] + 1).astype(jnp.float32)
    scale_table = (0.75 * next_block + 0.2 * far_block) / math.sqrt(WSN)

    def one_section(index):
        section_key = jax.random.fold_in(key, index)
        noise = jnp.clip(jax.random.normal(section_key, (SA, SA), jnp.float32), -4.0, 4.0)
        return (noise * scale_table).astype(jnp.bfloat16)
    return lax.map(one_section, jnp.arange(NSEP)).reshape(NSEP * SA, SA)


def draw_leaf_subtree(key, part):
    devices = LEAVES // SN_DEV
    per_section = devices // NSEP

    def one_device(index):
        device_key = jax.random.fold_in(key, index)
        first_key, rest_key, order_key = jax.random.split(device_key, 3)
        first = jax.random.permutation(first_key, SPAN)
        others = jax.random.randint(rest_key, (SN_DEV - SPAN,), 0, SPAN)
        backward = jnp.concatenate([first, others])
        section = index // per_section
        backward = jnp.minimum(backward, section)
        backward = jax.random.permutation(order_key, backward)
        return section - backward
    return jax.vmap(one_device)(jnp.arange(devices)).reshape(LEAVES).astype(jnp.int32)


def with_ends(entries, own_key, smallest, largest):
    spot = [jax.random.randint(jax.random.fold_in(own_key, axis), (), 0, length) for axis, length in enumerate(entries.shape)]
    longest = entries.shape.index(max(entries.shape))
    next_to = spot[:longest] + [(spot[longest] + 1) % entries.shape[longest]] + spot[longest + 1:]
    return entries.at[tuple(spot)].set(smallest).at[tuple(next_to)].set(largest)


def levels(stream_key, extent, cuts, least, high):
    def one(axis_at, blocks):
        draws = jax.random.uniform(jax.random.fold_in(jax.random.fold_in(stream_key, 6), axis_at), (blocks,), jnp.float32, least / len(cuts), high / len(cuts))
        return jnp.repeat(jnp.exp(draws), extent[axis_at] // blocks).reshape((-1,) + (1,) * (len(extent) - axis_at - 1))

    gain = one(*cuts[0])
    for cut in cuts[1:]:
        gain = gain * one(*cut)
    return gain


def scatter_about(own_key, extent, scale, limit, cuts=(), kind=jnp.bfloat16):
    drawn = jax.random.normal(own_key, extent, jnp.float32) * scale
    if len(cuts) > 0:
        drawn = levels(own_key, extent, cuts, -0.22, 0.18) * drawn
    return jnp.clip(drawn, min=-limit, max=limit).astype(kind)


def setup_inputs(seed: int = 0) -> dict:
    keys = jax.random.split(jax.random.key(seed), 9)
    return {
        "leaf_right": scatter_about(keys[0], (LEAVES, W, R), 1.0, 6.0, ((0, 32),)),
        "leaf_inverse": draw_leaf_inverse(jax.random.fold_in(keys[8], 71), 0),
        "panels": scatter_about(keys[2], (LEAVES, KB * BLK, W), (4 * W) ** -0.5, 0.125, ((0, 32),)),
        "leaf_subtree": draw_leaf_subtree(jax.random.fold_in(keys[8], 71), 0),
        "panel_block": with_ends(jax.random.randint(keys[4], (LEAVES, KB), 0, NBS), jax.random.fold_in(keys[4], 1), 0, NBS - 1).astype(jnp.int32),
        "separator_right": scatter_about(keys[5], (NSEP * SA, R), 1.0, 6.0, ((0, 32),)),
        "separator_inverse": draw_separator_inverse(jax.random.fold_in(keys[8], 71), 0),
        "separator_factor": draw_separator_factor(jax.random.fold_in(keys[8], 71), 0),
    }


def solve_leaves(inverse, right):
    return jnp.einsum("jab,jbr->jar", inverse.astype(jnp.float32), right.astype(jnp.float32)).astype(jnp.bfloat16)


def sweep_section(section_args):
    rhs, inverse, factor = section_args
    count = SA // WSN
    forward_blocks = []
    for column in range(count):
        first = column * WSN
        running = rhs[first:first + WSN].astype(jnp.float32)
        if column > 0:
            earlier = jnp.concatenate(forward_blocks, 0)
            running = running - jnp.dot(factor[first:first + WSN, :first], earlier, preferred_element_type=jnp.float32)
        forward_blocks.append(jnp.dot(inverse[first:first + WSN].astype(jnp.float32), running, precision=lax.Precision.HIGHEST, preferred_element_type=jnp.float32).astype(jnp.bfloat16))
    backward_blocks = [None] * count
    for column in reversed(range(count)):
        first = column * WSN
        running = forward_blocks[column].astype(jnp.float32)
        if column < count - 1:
            later = jnp.concatenate(backward_blocks[column + 1:], 0)
            running = running - lax.dot_general(factor[first + WSN:, first:first + WSN], later, (((0,), (0,)), ((), ())), preferred_element_type=jnp.float32)
        backward_blocks[column] = lax.dot_general(inverse[first:first + WSN].astype(jnp.float32), running, (((0,), (0,)), ((), ())), precision=lax.Precision.HIGHEST, preferred_element_type=jnp.float32).astype(jnp.bfloat16)
    return jnp.concatenate(backward_blocks, 0)


def reference(leaf_right, leaf_inverse, panels, leaf_subtree, panel_block, separator_right, separator_inverse, separator_factor):
    groups = leaf_right.shape[0] // SN_DEV
    row_blocks = SA // BLK
    targets_all = (leaf_subtree[:, None] * row_blocks + panel_block).astype(jnp.int32).reshape(groups, SN_DEV * KB)
    inputs = (leaf_right.reshape(groups, SN_DEV, W, R), leaf_inverse.reshape(groups, SN_DEV, W, W), panels.reshape(groups, SN_DEV, KB * BLK, W), targets_all)

    def forward_step(sums, group):
        right, inverse, panel_group, targets = group
        solved = solve_leaves(inverse, right)
        updates = jnp.einsum("jib,jbr->jir", panel_group.astype(jnp.float32), solved.astype(jnp.float32))
        return sums.at[targets].add(updates.reshape(SN_DEV * KB, BLK, R)), jnp.zeros((), jnp.float32)

    sums, unused = lax.scan(forward_step, jnp.zeros((NSEP * row_blocks, BLK, R), jnp.float32), inputs)
    separator_rhs = (separator_right.astype(jnp.float32) - sums.reshape(NSEP * SA, R)).astype(jnp.bfloat16)
    separator_x = lax.map(sweep_section, (separator_rhs.reshape(NSEP, SA, R), separator_inverse.reshape(NSEP, SA, WSN), separator_factor.reshape(NSEP, SA, SA)))
    solution_blocks = separator_x.reshape(NSEP * row_blocks, BLK, R)

    def backward_step(carry, group):
        right, inverse, panel_group, targets = group
        solved = solve_leaves(inverse, right)
        pieces = jnp.take(solution_blocks, targets, axis=0).reshape(SN_DEV, KB * BLK, R)
        reduced = jnp.einsum("jib,jir->jbr", panel_group.astype(jnp.float32), pieces.astype(jnp.float32))
        inner_rhs = (solved.astype(jnp.float32) - reduced).astype(jnp.bfloat16)
        result = jnp.einsum("jab,jar->jbr", inverse.astype(jnp.float32), inner_rhs.astype(jnp.float32)).astype(jnp.bfloat16)
        return carry, result

    unused_carry, leaf_solution = lax.scan(backward_step, jnp.zeros((), jnp.float32), inputs)
    return leaf_solution.reshape(groups * SN_DEV, W, R), separator_x.reshape(NSEP * SA, R)
```

```python
import functools

import jax
import jax.numpy as jnp
from jax import lax
from jax.experimental import pallas as pl
from jax.experimental.pallas import tpu as pltpu
from jax.sharding import PartitionSpec as P

WSN = 512
SA = 4096
R = 256
BLK = 64
KB = 4
SPAN = 3
MESH = pl.DeviceIdType.MESH
F32 = jnp.float32
BF16 = jnp.bfloat16


def mm(a, b):
    return jnp.dot(a, b, preferred_element_type=F32)


def mm_t(a, b):
    return lax.dot_general(a, b, (((0,), (0,)), ((), ())), preferred_element_type=F32)


def halves(v):
    hi = v.astype(BF16)
    return hi, (v - hi.astype(F32)).astype(BF16)


def kernel(
    S, M,
    right_h, inv_h, panels_h, meta_v, meta_s, sright_h, sinv_h, fac_h,
    ox, osx,
    rt, iv, pn, srt, sinv, fac,
    ly, ub, ucat, usnd, mr, ms,
    accs, accm, pr, ysnd, yrcv, run, yb, runt, xt, trcv, tsnd, xb, pcs, psnd, lo,
    lsem, msem, osem,
    u_ss, u_rs, m_ss, m_rs, p_ss, p_rs, y_ss, y_rs, f_ss, f_rs, t_ss, t_rs,
    xd_ss, xd_rs, xu_ss, xu_rs, b_ss, b_rs,
):
    s = lax.axis_index("leaf")
    m = lax.axis_index("sub")
    c = lax.rem(m, 2)
    y = lax.div(m, 2)
    ny = M // 2
    nl = right_h.shape[0]
    SH = srt.shape[0]
    B = SH // WSN
    nbm = SH // BLK
    c1, c2 = nl - 1, nl - 2
    first = {1: 0, 2: c1}
    base = {1: nl, 2: nl + c1}
    width = {1: c1, 2: c2}
    nslots = nl + c1 + c2
    partner = (s, m + 1 - 2 * c)
    up = (s, m + 1)
    down = (s, m - 1)

    def remote(src, dst, ssem, rsem, dev):
        return pltpu.make_async_remote_copy(
            src_ref=src, dst_ref=dst, send_sem=ssem, recv_sem=rsem, device_id=dev, device_id_type=MESH
        )

    locals_in = [
        (right_h, rt, 0), (inv_h, iv, nl), (panels_h, pn, 2 * nl),
    ]
    for j in range(nl):
        for src, dst, at in locals_in:
            pltpu.make_async_copy(src.at[j], dst.at[j], lsem.at[at + j]).start()
    big = [
        pltpu.make_async_copy(sright_h, srt, lsem.at[3 * nl]),
        pltpu.make_async_copy(sinv_h, sinv, lsem.at[3 * nl + 1]),
        pltpu.make_async_copy(fac_h, fac, lsem.at[3 * nl + 2]),
    ]
    for copy in big:
        copy.start()

    barrier = pltpu.get_barrier_semaphore()

    def greet(dev):
        pl.semaphore_signal(barrier, inc=1, device_id=dev, device_id_type=MESH)

    def when_greet(cond, dev):
        pl.when(cond)(lambda: greet(dev))
        return cond.astype(jnp.int32)

    friends = when_greet(m > 0, down) + when_greet(m < M - 1, up)
    for i in range(1, ny):
        greet((s, lax.rem(y + i, ny) * 2 + c))
    for d in (1, 2):
        friends = friends + when_greet(s >= d, (s - d, m))
        friends = friends + when_greet(s + d < S, (s + d, m))

    @pl.loop(0, nl)
    def _(j):
        for src, dst, at in locals_in:
            pltpu.make_async_copy(src.at[j], dst.at[j], lsem.at[at + j]).wait()
        sol = mm(iv[j], rt[j]).astype(BF16)
        ly[j] = sol
        ub[j] = mm(pn[j], sol).astype(BF16)

    def slots(read, sec):
        dist = [sec - read(j, KB) for j in range(nl)]
        rank = []
        for j in range(nl):
            r = jnp.int32(0)
            for i in range(j):
                r = r + (dist[i] == dist[j]).astype(jnp.int32)
            rank.append(r)
        return dist, rank

    own = lambda j, k: meta_s[j, k]
    dist, rank = slots(own, s)

    pl.semaphore_wait(barrier, friends + (ny - 1))

    def metas(d):
        return remote(meta_v, mr.at[d - 1], m_ss.at[d - 1], m_rs.at[d - 1], (s - d, m))

    def updates(d, third):
        if third:
            a, b = usnd.at[2], ucat.at[2]
            return remote(a, b, u_ss.at[2], u_rs.at[2], (s - d, m))
        a = usnd.at[pl.ds(first[d], 2)]
        b = ucat.at[pl.ds(first[d], 2)]
        return remote(a, b, u_ss.at[d - 1], u_rs.at[d - 1], (s - d, m))

    for d in (2, 1):
        @pl.when(s >= d)
        def _():
            metas(d).start()
            for q in range(width[d]):
                pick = jnp.int32(0)
                for j in range(nl):
                    pick = jnp.where((dist[j] == d) & (rank[j] == q), j, pick)
                usnd[first[d] + q] = ub[pick]
            updates(d, False).start()
    pl.when(s == 1)(lambda: updates(1, True).start())

    for d in (1, 2):
        @pl.when(s + d < S)
        def _():
            metas(d).wait_recv()

        @pl.when(s + d >= S)
        def _():
            mr[d - 1] = jnp.full(mr.shape[1:], -1000, jnp.int32)
            ucat[first[d]:first[d] + 2] = jnp.zeros((2, KB * BLK, R), BF16)

        @pl.when(s < d)
        def _():
            pcs[base[d]:base[d] + 2] = jnp.zeros((2, KB * BLK, R), BF16)
        copy = pltpu.make_async_copy(mr.at[d - 1], ms.at[d - 1], msem.at[d - 1])
        copy.start()
        copy.wait()

    @pl.when(s > 0)
    def _():
        ucat[2] = jnp.zeros((KB * BLK, R), BF16)

    @pl.when(s != 1)
    def _():
        pcs[nl + 2] = jnp.zeros((KB * BLK, R), BF16)

    targets = []
    for j in range(nl):
        targets.append([jnp.where(dist[j] == 0, meta_s[j, k], -1) for k in range(KB)])
    for d in (1, 2):
        read = lambda j, k, d=d: ms[d - 1, j, k]
        rd, rr = slots(read, s + d)
        for q in range(width[d]):
            entry = []
            for k in range(KB):
                t = jnp.int32(-1)
                for j in range(nl):
                    t = jnp.where((rd[j] == d) & (rr[j] == q), read(j, k), t)
                entry.append(t)
            targets.append(entry)

    lane = lax.broadcasted_iota(jnp.int32, (1, KB * BLK), 1)
    rows_of = []
    for entry in targets:
        v = jnp.full((1, KB * BLK), entry[KB - 1] * BLK, jnp.int32)
        for k in range(KB - 1):
            v = jnp.where(lane // BLK == k, entry[k] * BLK, v)
        rows_of.append(v + lane % BLK)

    for d in (1, 2):
        pl.when(s + d < S)(lambda d=d: updates(d, False).wait_recv())
    pl.when(s == 0)(lambda: updates(1, True).wait_recv())

    def scatter(member, put):
        @pl.loop(0, SH // 256)
        def _(i):
            at = member * SH + i * 256
            iota = lax.broadcasted_iota(jnp.int32, (256, KB * BLK), 0) + at
            total = jnp.zeros((256, R), F32)
            for n in range(nslots):
                pick = jnp.where(iota == rows_of[n], 1.0, 0.0).astype(BF16)
                total = total + mm(pick, ub[n] if n < nl else ucat[n - nl])
            put(pl.ds(pl.multiple_of(i * 256, 256), 256), total)

    def pair(at):
        return remote(accs.at[at], pr.at[at], p_ss.at[at], p_rs.at[at], partner)

    def across(to, frm):
        return remote(ysnd.at[to], yrcv.at[frm], y_ss.at[to], y_rs.at[frm], (s, to * 2 + c))

    order = [lax.rem(y + i, ny) for i in range(1, ny)] + [y]
    for o in order:
        def put(rows, total, o=o):
            accs[o, rows, :] = total.astype(BF16)
        scatter(o * 2 + 1 - c, put)
        pair(o).start()
    for n, o in enumerate(order):
        def put(rows, total, o=o):
            accm[o, rows, :] = total
        scatter(o * 2 + c, put)
        pair(o).wait_recv()
        if n < ny - 1:
            ysnd[o] = (accm[o] + pr[o].astype(F32)).astype(BF16)
            across(o, y).start()
    big[0].wait()
    run[...] = srt[...].astype(F32) - accm[y] - pr[y].astype(F32)
    for o in order[:-1]:
        across(o, o).wait_recv()
        run[...] -= yrcv[o].astype(F32)
    run[...] = run[...].astype(BF16).astype(F32)
    big[1].wait()
    big[2].wait()

    def cols(p, q=0, n=None):
        return pl.ds(pl.multiple_of(p * SH + q * WSN, WSN), SH if n is None else n)

    def forward(p):
        return remote(yb.at[p], yb.at[p], f_ss.at[p], f_rs.at[p], up)

    @pl.loop(0, m)
    def _(p):
        forward(p).wait_recv()
        pl.when(m < M - 1)(lambda: forward(p).start())
        for b in range(B):
            at = pl.ds(b * WSN, WSN)
            run[at, :] -= mm(fac[at, cols(p)], yb[p])

    for b in range(B):
        at = pl.ds(b * WSN, WSN)
        bracket = run[at, :]
        for e in range(b):
            bracket = bracket - mm(fac[at, cols(m, e, WSN)], yb[m, pl.ds(e * WSN, WSN), :])
        hi, low = halves(bracket)
        block = (mm(sinv[at, :], hi) + mm(sinv[at, :], low)).astype(BF16)
        yb[m, at, :] = block
    pl.when(m < M - 1)(lambda: forward(m).start())
    for b in range(B):
        at = pl.ds(b * WSN, WSN)
        runt[:, at] = yb[m, at, :].astype(F32).T

    def back(p):
        return remote(tsnd.at[p], trcv.at[p], t_ss.at[p], t_rs.at[p], down)

    @pl.when(m < M - 1)
    def _():
        back(m).wait_recv()
        runt[...] -= trcv[m].astype(F32)

    for b in reversed(range(B)):
        at = pl.ds(b * WSN, WSN)
        bracket = runt[:, at]
        for e in range(b + 1, B):
            rows = pl.ds(e * WSN, WSN)
            bracket = bracket - mm(xt[:, rows], fac[rows, cols(m, b, WSN)])
        hi, low = halves(bracket)
        xt[:, at] = (mm(hi, sinv[at, :]) + mm(low, sinv[at, :])).astype(BF16)

    @pl.loop(0, m)
    def _(i):
        p = m - 1 - i
        pl.when(m < M - 1)(lambda: back(p).wait_recv())
        for b in range(B):
            at = pl.ds(b * WSN, WSN)
            term = mm(xt[...], fac[:, cols(p, b, WSN)])
            before = jnp.where(m < M - 1, trcv[p, :, at].astype(F32), 0.0)
            tsnd[p, :, at] = (term + before).astype(BF16)
        back(p).start()

    for b in range(B):
        block = xt[:, b * WSN:(b + 1) * WSN].astype(F32).T.astype(BF16)
        xb[pl.ds(m * nbm + b * (WSN // BLK), WSN // BLK)] = block.reshape(WSN // BLK, BLK, R)

    def xdown(p):
        part = xb.at[pl.ds(p * nbm, nbm)]
        return remote(part, part, xd_ss.at[p], xd_rs.at[p], down)

    def xup(p):
        part = xb.at[pl.ds(p * nbm, nbm)]
        return remote(part, part, xu_ss.at[p], xu_rs.at[p], up)

    pl.when(m < M - 1)(lambda: xup(m).start())
    pl.when(m > 0)(lambda: xdown(m).start())
    out_sep = pltpu.make_async_copy(xb.at[pl.ds(m * nbm, nbm)], osx, osem.at[nl])
    out_sep.start()

    @pl.loop(m + 1, M)
    def _(p):
        xdown(p).wait_recv()
        pl.when(m > 0)(lambda: xdown(p).start())

    @pl.loop(0, m)
    def _(i):
        p = m - 1 - i
        xup(p).wait_recv()
        pl.when(m < M - 1)(lambda: xup(p).start())

    def pieces(d, third):
        if third:
            return remote(psnd.at[2], pcs.at[nl + 2], b_ss.at[2], b_rs.at[2], (s + d, m))
        a = psnd.at[pl.ds(first[d], 2)]
        b = pcs.at[pl.ds(base[d], 2)]
        return remote(a, b, b_ss.at[d - 1], b_rs.at[d - 1], (s + d, m))

    for d in (2, 1):
        @pl.when(s + d < S)
        def _():
            for q in range(width[d]):
                for k in range(KB):
                    t = jnp.maximum(targets[base[d] + q][k], 0)
                    psnd[first[d] + q, k * BLK:(k + 1) * BLK, :] = xb[t]
            pieces(d, False).start()
    pl.when(s == 0)(lambda: pieces(1, True).start())
    for j in range(nl):
        for k in range(KB):
            pcs[j, k * BLK:(k + 1) * BLK, :] = xb[meta_s[j, k]]
    for d in (1, 2):
        pl.when(s >= d)(lambda d=d: pieces(d, False).wait_recv())
    pl.when(s == 1)(lambda: pieces(1, True).wait_recv())

    for j in range(nl):
        at = jnp.where(dist[j] == 0, j, jnp.where(dist[j] == 1, nl + rank[j], nl + c1 + rank[j]))
        at = jnp.clip(at, 0, nslots - 1)
        reduced = mm_t(pn[j], pcs[at])
        inner = (ly[j].astype(F32) - reduced).astype(BF16)
        lo[j] = mm_t(iv[j], inner).astype(BF16)
        pltpu.make_async_copy(lo.at[j], ox.at[j], osem.at[j]).start()

    for d in (1, 2):
        @pl.when(s >= d)
        def _():
            metas(d).wait_send()
            updates(d, False).wait_send()

        pl.when(s + d < S)(lambda d=d: pieces(d, False).wait_send())
    pl.when(s == 1)(lambda: updates(1, True).wait_send())
    pl.when(s == 0)(lambda: pieces(1, True).wait_send())
    for o in order:
        pair(o).wait_send()
    for o in order[:-1]:
        across(o, y).wait_send()

    @pl.when(m < M - 1)
    def _():
        @pl.loop(0, m + 1)
        def _(p):
            forward(p).wait_send()
            xup(p).wait_send()

    @pl.when(m > 0)
    def _():
        @pl.loop(0, m)
        def _(p):
            back(p).wait_send()

        @pl.loop(m, M)
        def _(p):
            xdown(p).wait_send()

    out_sep.wait()
    for j in range(nl):
        pltpu.make_async_copy(lo.at[j], ox.at[j], osem.at[j]).wait()


def shards(S, M, leaf_right, leaf_inverse, panels, leaf_subtree, panel_block, separator_right, separator_inverse, separator_factor):
    nl, W = leaf_right.shape[:2]
    SH = separator_right.shape[0]
    ny = M // 2
    nbm = SH // BLK
    nslots = 3 * nl - 3
    meta = jnp.concatenate([panel_block, leaf_subtree[:, None]], axis=1)
    meta = jnp.pad(meta, ((0, 8 - nl), (0, 128 - KB - 1)))
    anywhere = pl.BlockSpec(memory_space=pl.ANY)
    V = pltpu.VMEM
    D = pltpu.SemaphoreType.DMA
    scratch = [
        V((nl, W, R), BF16), V((nl, W, W), BF16), V((nl, KB * BLK, W), BF16),
        V((SH, R), BF16), V((SH, WSN), BF16), V((SH, SA), BF16),
        V((nl, W, R), BF16), V((nl, KB * BLK, R), BF16), V((2 * nl - 3, KB * BLK, R), BF16), V((2 * nl - 3, KB * BLK, R), BF16),
        V((2, 8, 128), jnp.int32), pltpu.SMEM((2, 8, 128), jnp.int32),
        V((ny, SH, R), BF16), V((ny, SH, R), F32), V((ny, SH, R), BF16), V((ny, SH, R), BF16), V((ny, SH, R), BF16),
        V((SH, R), F32), V((M, SH, R), BF16), V((R, SH), F32), V((R, SH), BF16),
        V((M, R, SH), BF16), V((M, R, SH), BF16), V((SA // BLK, BLK, R), BF16),
        V((nslots, KB * BLK, R), BF16), V((2 * nl - 3, KB * BLK, R), BF16), V((nl, W, R), BF16),
        D((3 * nl + 3,)), D((2,)), D((nl + 1,)),
        D((3,)), D((3,)), D((2,)), D((2,)), D((ny,)), D((ny,)), D((ny,)), D((ny,)),
        D((M,)), D((M,)), D((M,)), D((M,)), D((M,)), D((M,)), D((M,)), D((M,)), D((3,)), D((3,)),
    ]
    leaf_x, sep_x = pl.pallas_call(
        functools.partial(kernel, S, M),
        out_shape=(
            jax.ShapeDtypeStruct((nl, W, R), BF16),
            jax.ShapeDtypeStruct((nbm, BLK, R), BF16),
        ),
        in_specs=[
            anywhere, anywhere, anywhere,
            pl.BlockSpec(memory_space=pltpu.VMEM), pl.BlockSpec(memory_space=pltpu.SMEM),
            anywhere, anywhere, anywhere,
        ],
        out_specs=(anywhere, anywhere),
        scratch_shapes=scratch,
        compiler_params=pltpu.CompilerParams(
            collective_id=0, has_side_effects=True, vmem_limit_bytes=56 * 1024 * 1024
        ),
        cost_estimate=pl.CostEstimate(flops=12_000_000_000, bytes_accessed=16_000_000, transcendentals=0),
    )(leaf_right, leaf_inverse, panels, meta, meta, separator_right, separator_inverse, separator_factor)
    return leaf_x, sep_x.reshape(SH, R)


def solution(mesh):
    placed = (
        P(("leaf", "sub"), None, None),
        P(("leaf", "sub"), None, None),
        P(("leaf", "sub"), None, None),
        P(("leaf", "sub")),
        P(("leaf", "sub"), None),
        P(("leaf", "sub"), None),
        P(("leaf", "sub"), None),
        P(("leaf", "sub"), None),
    )
    return jax.shard_map(
        functools.partial(shards, mesh.shape["leaf"], mesh.shape["sub"]),
        mesh=mesh,
        in_specs=placed,
        out_specs=(P(("leaf", "sub"), None, None), P(("leaf", "sub"), None)),
        check_vma=False,
    )
```

```python
import functools

import jax
import jax.numpy as jnp
from jax import lax
from jax.experimental import pallas as pl
from jax.experimental.pallas import tpu as pltpu
from jax.sharding import PartitionSpec as P

WSN = 512
SA = 4096
R = 256
BLK = 64
KB = 4
SPAN = 3
MESH = pl.DeviceIdType.MESH
F32 = jnp.float32
BF16 = jnp.bfloat16


def mm(a, b):
    return jnp.dot(a, b, preferred_element_type=F32)


def mm_t(a, b):
    return lax.dot_general(a, b, (((0,), (0,)), ((), ())), preferred_element_type=F32)


def halves(v):
    hi = v.astype(BF16)
    return hi, (v - hi.astype(F32)).astype(BF16)


def kernel(
    S, M,
    right_h, inv_h, panels_h, block_s, tree_s, sright_h, sinv_h, fac_h,
    ox, osx,
    rt, iv, pn, srt, sinv, fac,
    ivt, pnt, ly, ub, ucat, usnd, mv, mr, ms,
    accm, accs, pr, ysnd, yrcv, run, yb, runt, xt, trcv, tsnd, xb, pcs, psnd, lo,
    lsem, msem, osem,
    u_ss, u_rs, m_ss, m_rs, p_ss, p_rs, y_ss, y_rs, f_ss, f_rs, t_ss, t_rs,
    xd_ss, xd_rs, xu_ss, xu_rs, b_ss, b_rs,
):
    s = lax.axis_index("leaf")
    m = lax.axis_index("sub")
    c = lax.rem(m, 2)
    y = lax.div(m, 2)
    ny = M // 2
    nl = right_h.shape[0]
    SH = srt.shape[0]
    B = SH // WSN
    nbm = SH // BLK
    c1, c2 = nl - 1, nl - 2
    first = {1: 0, 2: c1}
    base = {1: nl, 2: nl + c1}
    width = {1: c1, 2: c2}
    nslots = nl + c1 + c2
    partner = (s, m + 1 - 2 * c)
    up = (s, m + 1)
    down = (s, m - 1)

    def remote(src, dst, ssem, rsem, dev):
        return pltpu.make_async_remote_copy(
            src_ref=src, dst_ref=dst, send_sem=ssem, recv_sem=rsem, device_id=dev, device_id_type=MESH
        )

    locals_in = [
        (right_h, rt, 0), (inv_h, iv, nl), (panels_h, pn, 2 * nl),
    ]
    for j in range(nl):
        for src, dst, at in locals_in:
            pltpu.make_async_copy(src.at[j], dst.at[j], lsem.at[at + j]).start()
    big = [
        pltpu.make_async_copy(sright_h, srt, lsem.at[3 * nl]),
        pltpu.make_async_copy(sinv_h, sinv, lsem.at[3 * nl + 1]),
        pltpu.make_async_copy(fac_h, fac, lsem.at[3 * nl + 2]),
    ]
    for copy in big:
        copy.start()

    barrier = pltpu.get_barrier_semaphore()

    def greet(dev):
        pl.semaphore_signal(barrier, inc=1, device_id=dev, device_id_type=MESH)

    def when_greet(cond, dev):
        pl.when(cond)(lambda: greet(dev))
        return cond.astype(jnp.int32)

    friends = when_greet(m > 0, down) + when_greet(m < M - 1, up)
    for i in range(1, ny):
        greet((s, lax.rem(y + i, ny) * 2 + c))
    for d in (1, 2):
        friends = friends + when_greet(s >= d, (s - d, m))
        friends = friends + when_greet(s + d < S, (s + d, m))

    @pl.loop(0, nl)
    def _(j):
        for src, dst, at in locals_in:
            pltpu.make_async_copy(src.at[j], dst.at[j], lsem.at[at + j]).wait()
        sol = mm(iv[j], rt[j]).astype(BF16)
        ly[j] = sol
        ub[j] = mm(pn[j], sol).astype(BF16)

    def slots(read, sec):
        dist = [sec - read(j, KB) for j in range(nl)]
        rank = []
        for j in range(nl):
            r = jnp.int32(0)
            for i in range(j):
                r = r + (dist[i] == dist[j]).astype(jnp.int32)
            rank.append(r)
        return dist, rank

    own = lambda j, k: tree_s[j] if k == KB else block_s[j, k]
    sub = lax.broadcasted_iota(jnp.int32, mv.shape, 0)
    lane = lax.broadcasted_iota(jnp.int32, mv.shape, 1)
    meta = jnp.zeros(mv.shape, jnp.int32)
    for j in range(nl):
        for k in range(KB + 1):
            meta = jnp.where((sub == j) & (lane == k), own(j, k), meta)
    mv[...] = meta
    dist, rank = slots(own, s)

    pl.semaphore_wait(barrier, friends + (ny - 1))

    def metas(d):
        return remote(mv, mr.at[d - 1], m_ss.at[d - 1], m_rs.at[d - 1], (s - d, m))

    def updates(d, third):
        if third:
            a, b = usnd.at[2], ucat.at[2]
            return remote(a, b, u_ss.at[2], u_rs.at[2], (s - d, m))
        a = usnd.at[pl.ds(first[d], 2)]
        b = ucat.at[pl.ds(first[d], 2)]
        return remote(a, b, u_ss.at[d - 1], u_rs.at[d - 1], (s - d, m))

    for d in (2, 1):
        @pl.when(s >= d)
        def _():
            metas(d).start()
            for q in range(width[d]):
                pick = jnp.int32(0)
                for j in range(nl):
                    pick = jnp.where((dist[j] == d) & (rank[j] == q), j, pick)
                usnd[first[d] + q] = ub[pick]
            updates(d, False).start()
    pl.when(s == 1)(lambda: updates(1, True).start())

    def row_ids(entry):
        lane = lax.broadcasted_iota(jnp.int32, (1, KB * BLK), 1)
        v = jnp.full((1, KB * BLK), entry[KB - 1] * BLK, jnp.int32)
        for k in range(KB - 1):
            v = jnp.where(lane // BLK == k, entry[k] * BLK, v)
        return v + lane % BLK

    def scatter(begin, blocks, pairs, put):
        @pl.loop(0, blocks)
        def _(i):
            at = begin + i * 256
            iota = lax.broadcasted_iota(jnp.int32, (256, KB * BLK), 0) + at
            total = jnp.zeros((256, R), F32)
            for ids, ref, n in pairs:
                pick = jnp.where(iota == ids, 1.0, 0.0).astype(BF16)
                total = total + mm(pick, ref[n])
            put(pl.ds(pl.multiple_of(at, 256), 256), total)

    targets = []
    for j in range(nl):
        targets.append([jnp.where(dist[j] == 0, block_s[j, k], -1) for k in range(KB)])
    pairs = [(row_ids(targets[j]), ub, j) for j in range(nl)]

    def put_own(rows, total):
        accm[rows, :] = total
    scatter(0, SA // 256, pairs, put_own)

    @pl.loop(0, nl)
    def _(j):
        ivt[j] = iv[j].astype(F32).T.astype(BF16)
        pnt[j] = pn[j].astype(F32).T.astype(BF16)

    for d in (1, 2):
        @pl.when(s + d < S)
        def _():
            metas(d).wait_recv()

        @pl.when(s + d >= S)
        def _():
            mr[d - 1] = jnp.full(mr.shape[1:], -1000, jnp.int32)
            ucat[first[d]:first[d] + 2] = jnp.zeros((2, KB * BLK, R), BF16)

        @pl.when(s < d)
        def _():
            pcs[base[d]:base[d] + 2] = jnp.zeros((2, KB * BLK, R), BF16)
        copy = pltpu.make_async_copy(mr.at[d - 1], ms.at[d - 1], msem.at[d - 1])
        copy.start()
        copy.wait()

    @pl.when(s > 0)
    def _():
        ucat[2] = jnp.zeros((KB * BLK, R), BF16)

    @pl.when(s != 1)
    def _():
        pcs[nl + 2] = jnp.zeros((KB * BLK, R), BF16)

    pairs = []
    for d in (1, 2):
        read = lambda j, k, d=d: ms[d - 1, j, k]
        rd, rr = slots(read, s + d)
        for q in range(width[d]):
            entry = []
            for k in range(KB):
                t = jnp.int32(-1)
                for j in range(nl):
                    t = jnp.where((rd[j] == d) & (rr[j] == q), read(j, k), t)
                entry.append(t)
            targets.append(entry)
            pairs.append((row_ids(entry), ucat, first[d] + q))
    third = pairs.pop(2)

    for d in (1, 2):
        pl.when(s + d < S)(lambda d=d: updates(d, False).wait_recv())

    def put_more(rows, total):
        accm[rows, :] += total

    @pl.when(s == 0)
    def _():
        updates(1, True).wait_recv()
        scatter(0, SA // 256, [third], put_more)

    def pair(o, b):
        return remote(accs.at[o, b], pr.at[o, b], p_ss.at[o, b], p_rs.at[o, b], partner)

    def across(to, frm, b):
        return remote(ysnd.at[to, b], yrcv.at[frm, b], y_ss.at[to, b], y_rs.at[frm, b], (s, to * 2 + c))

    def rows_at(o, core, b):
        return pl.ds(pl.multiple_of((o * 2 + core) * SH + b * WSN, WSN), WSN)

    def more(o, core, b):
        scatter((o * 2 + core) * SH + b * WSN, WSN // 256, pairs, put_more)

    order = [lax.rem(y + i, ny) for i in range(1, ny)] + [y]
    for o in order:
        for b in range(B):
            more(o, 1 - c, b)
            accs[o, b] = accm[rows_at(o, 1 - c, b), :].astype(BF16)
            pair(o, b).start()
        for b in range(B):
            more(o, c, b)
            if o is not y:
                pair(o, b).wait_recv()
                ysnd[o, b] = (accm[rows_at(o, c, b), :] + pr[o, b].astype(F32)).astype(BF16)
                across(o, y, b).start()
    big[0].wait()
    big[1].wait()
    big[2].wait()

    def right_side(b):
        at = pl.ds(b * WSN, WSN)
        pair(y, b).wait_recv()
        side = srt[at, :].astype(F32) - accm[rows_at(y, c, b), :] - pr[y, b].astype(F32)
        for o in order[:-1]:
            across(o, o, b).wait_recv()
            side = side - yrcv[o, b].astype(F32)
        run[at, :] = side.astype(BF16).astype(F32)

    def cols(q):
        return pl.ds(pl.multiple_of(q * WSN, WSN), WSN)

    def forward(q):
        return remote(yb.at[q], yb.at[q], f_ss.at[q], f_rs.at[q], up)

    @pl.when(m > 0)
    def _():
        for b in range(B):
            right_side(b)

    @pl.loop(0, m * B)
    def _(q):
        forward(q).wait_recv()
        pl.when(m < M - 1)(lambda: forward(q).start())
        for b in range(B):
            at = pl.ds(b * WSN, WSN)
            run[at, :] -= mm(fac[at, cols(q)], yb[q])

    for b in range(B):
        at = pl.ds(b * WSN, WSN)
        pl.when(m == 0)(lambda b=b: right_side(b))
        bracket = run[at, :]
        for e in range(b):
            bracket = bracket - mm(fac[at, cols(m * B + e)], yb[m * B + e])
        hi, low = halves(bracket)
        yb[m * B + b] = (mm(sinv[at, :], hi) + mm(sinv[at, :], low)).astype(BF16)
        pl.when(m < M - 1)(lambda b=b: forward(m * B + b).start())
    for b in range(B):
        runt[:, b * WSN:(b + 1) * WSN] = yb[m * B + b].astype(F32).T

    def back(q):
        return remote(tsnd.at[q], trcv.at[q], t_ss.at[q], t_rs.at[q], down)

    nbs = WSN // BLK

    def xdown(q):
        part = xb.at[pl.ds(q * nbs, nbs)]
        return remote(part, part, xd_ss.at[q], xd_rs.at[q], down)

    def xup(q):
        part = xb.at[pl.ds(q * nbs, nbs)]
        return remote(part, part, xu_ss.at[q], xu_rs.at[q], up)

    def send_x(b):
        block = xt[:, b * WSN:(b + 1) * WSN].astype(F32).T.astype(BF16)
        q = m * B + b
        xb[pl.ds(q * nbs, nbs)] = block.reshape(nbs, BLK, R)
        pl.when(m < M - 1)(lambda: xup(q).start())
        pl.when(m > 0)(lambda: xdown(q).start())

    for b in reversed(range(B)):
        at = pl.ds(b * WSN, WSN)

        @pl.when(m < M - 1)
        def _():
            back(m * B + b).wait_recv()
            runt[:, at] -= trcv[m * B + b].astype(F32)
        bracket = runt[:, at]
        for e in range(b + 1, B):
            rows = pl.ds(e * WSN, WSN)
            bracket = bracket - mm(xt[:, rows], fac[rows, cols(m * B + b)])
        hi, low = halves(bracket)
        xt[:, at] = (mm(hi, sinv[at, :]) + mm(low, sinv[at, :])).astype(BF16)
        pl.when(m == 0)(lambda b=b: send_x(b))

    @pl.loop(0, m * B)
    def _(i):
        q = m * B - 1 - i
        pl.when(m < M - 1)(lambda: back(q).wait_recv())
        term = mm(xt[...], fac[:, cols(q)])
        before = jnp.where(m < M - 1, trcv[q].astype(F32), 0.0)
        tsnd[q] = (term + before).astype(BF16)
        back(q).start()

    @pl.when(m > 0)
    def _():
        @pl.loop(0, m * B)
        def _(q):
            back(q).wait_send()
        for b in reversed(range(B)):
            send_x(b)

    out_sep = pltpu.make_async_copy(xb.at[pl.ds(m * nbm, nbm)], osx, osem.at[nl])
    out_sep.start()

    @pl.loop(0, (M - 1 - m) * B)
    def _(i):
        q = M * B - 1 - i
        xdown(q).wait_recv()
        pl.when(m > 0)(lambda: xdown(q).start())

    @pl.loop(0, m * B)
    def _(i):
        q = m * B - 1 - i
        xup(q).wait_recv()
        pl.when(m < M - 1)(lambda: xup(q).start())

    def pieces(d, third):
        if third:
            return remote(psnd.at[2], pcs.at[nl + 2], b_ss.at[2], b_rs.at[2], (s + d, m))
        a = psnd.at[pl.ds(first[d], 2)]
        b = pcs.at[pl.ds(base[d], 2)]
        return remote(a, b, b_ss.at[d - 1], b_rs.at[d - 1], (s + d, m))

    for d in (2, 1):
        @pl.when(s + d < S)
        def _():
            for q in range(width[d]):
                for k in range(KB):
                    t = jnp.maximum(targets[base[d] + q][k], 0)
                    psnd[first[d] + q, k * BLK:(k + 1) * BLK, :] = xb[t]
            pieces(d, False).start()
    pl.when(s == 0)(lambda: pieces(1, True).start())
    for j in range(nl):
        for k in range(KB):
            pcs[j, k * BLK:(k + 1) * BLK, :] = xb[block_s[j, k]]
    for d in (1, 2):
        pl.when(s >= d)(lambda d=d: pieces(d, False).wait_recv())
    pl.when(s == 1)(lambda: pieces(1, True).wait_recv())

    for j in range(nl):
        at = jnp.where(dist[j] == 0, j, jnp.where(dist[j] == 1, nl + rank[j], nl + c1 + rank[j]))
        at = jnp.clip(at, 0, nslots - 1)
        reduced = mm(pnt[j], pcs[at])
        inner = (ly[j].astype(F32) - reduced).astype(BF16)
        lo[j] = mm(ivt[j], inner).astype(BF16)
        pltpu.make_async_copy(lo.at[j], ox.at[j], osem.at[j]).start()

    for d in (1, 2):
        @pl.when(s >= d)
        def _():
            metas(d).wait_send()
            updates(d, False).wait_send()

        pl.when(s + d < S)(lambda d=d: pieces(d, False).wait_send())
    pl.when(s == 1)(lambda: updates(1, True).wait_send())
    pl.when(s == 0)(lambda: pieces(1, True).wait_send())
    for o in order:
        for b in range(B):
            pair(o, b).wait_send()
            if o is not y:
                across(o, y, b).wait_send()

    @pl.when(m < M - 1)
    def _():
        @pl.loop(0, (m + 1) * B)
        def _(q):
            forward(q).wait_send()
            xup(q).wait_send()

    @pl.when(m > 0)
    def _():
        @pl.loop(m * B, M * B)
        def _(q):
            xdown(q).wait_send()

    out_sep.wait()
    for j in range(nl):
        pltpu.make_async_copy(lo.at[j], ox.at[j], osem.at[j]).wait()


def shards(S, M, leaf_right, leaf_inverse, panels, leaf_subtree, panel_block, separator_right, separator_inverse, separator_factor):
    nl, W = leaf_right.shape[:2]
    SH = separator_right.shape[0]
    ny = M // 2
    nbm = SH // BLK
    B = SH // WSN
    N = SA // WSN
    nslots = 3 * nl - 3
    anywhere = pl.BlockSpec(memory_space=pl.ANY)
    V = pltpu.VMEM
    D = pltpu.SemaphoreType.DMA
    scratch = [
        V((nl, W, R), BF16), V((nl, W, W), BF16), V((nl, KB * BLK, W), BF16),
        V((SH, R), BF16), V((SH, WSN), BF16), V((SH, SA), BF16),
        V((nl, W, W), BF16), V((nl, W, KB * BLK), BF16),
        V((nl, W, R), BF16), V((nl, KB * BLK, R), BF16), V((2 * nl - 3, KB * BLK, R), BF16), V((2 * nl - 3, KB * BLK, R), BF16),
        V((8, 128), jnp.int32), V((2, 8, 128), jnp.int32), pltpu.SMEM((2, 8, 128), jnp.int32),
        V((SA, R), F32), V((ny, B, WSN, R), BF16), V((ny, B, WSN, R), BF16), V((ny, B, WSN, R), BF16), V((ny, B, WSN, R), BF16),
        V((SH, R), F32), V((N, WSN, R), BF16), V((R, SH), F32), V((R, SH), BF16),
        V((N, R, WSN), BF16), V((N, R, WSN), BF16), V((SA // BLK, BLK, R), BF16),
        V((nslots, KB * BLK, R), BF16), V((2 * nl - 3, KB * BLK, R), BF16), V((nl, W, R), BF16),
        D((3 * nl + 3,)), D((2,)), D((nl + 1,)),
        D((3,)), D((3,)), D((2,)), D((2,)), D((ny, B)), D((ny, B)), D((ny, B)), D((ny, B)),
        D((N,)), D((N,)), D((N,)), D((N,)), D((N,)), D((N,)), D((N,)), D((N,)), D((3,)), D((3,)),
    ]
    leaf_x, sep_x = pl.pallas_call(
        functools.partial(kernel, S, M),
        out_shape=(
            jax.ShapeDtypeStruct((nl, W, R), BF16),
            jax.ShapeDtypeStruct((nbm, BLK, R), BF16),
        ),
        in_specs=[
            anywhere, anywhere, anywhere,
            pl.BlockSpec(memory_space=pltpu.SMEM), pl.BlockSpec(memory_space=pltpu.SMEM),
            anywhere, anywhere, anywhere,
        ],
        out_specs=(anywhere, anywhere),
        scratch_shapes=scratch,
        compiler_params=pltpu.CompilerParams(
            collective_id=0, has_side_effects=True, vmem_limit_bytes=56 * 1024 * 1024
        ),
        cost_estimate=pl.CostEstimate(flops=12_000_000_000, bytes_accessed=16_000_000, transcendentals=0),
    )(leaf_right, leaf_inverse, panels, panel_block, leaf_subtree, separator_right, separator_inverse, separator_factor)
    return leaf_x, sep_x.reshape(SH, R)


def solution(mesh):
    placed = (
        P(("leaf", "sub"), None, None),
        P(("leaf", "sub"), None, None),
        P(("leaf", "sub"), None, None),
        P(("leaf", "sub")),
        P(("leaf", "sub"), None),
        P(("leaf", "sub"), None),
        P(("leaf", "sub"), None),
        P(("leaf", "sub"), None),
    )
    return jax.shard_map(
        functools.partial(shards, mesh.shape["leaf"], mesh.shape["sub"]),
        mesh=mesh,
        in_specs=placed,
        out_specs=(P(("leaf", "sub"), None, None), P(("leaf", "sub"), None)),
        check_vma=False,
    )
```

```python
import functools

import jax
import jax.numpy as jnp
from jax import lax
from jax.experimental import pallas as pl
from jax.experimental.pallas import tpu as pltpu
from jax.sharding import PartitionSpec as P

WSN = 512
SA = 4096
R = 256
BLK = 64
KB = 4
SPAN = 3
MESH = pl.DeviceIdType.MESH
F32 = jnp.float32
BF16 = jnp.bfloat16


def mm(a, b):
    return jnp.dot(a, b, preferred_element_type=F32)


def mm_t(a, b):
    return lax.dot_general(a, b, (((0,), (0,)), ((), ())), preferred_element_type=F32)


def kernel(
    S, M,
    right_h, inv_h, panels_h, block_s, tree_s, sright_h, sinv_h, fac_h,
    ox, osx,
    rt, iv, pn, srt, sinv, fac,
    ivt, pnt, ly, ub, ucat, usnd, mv, mr, ms,
    accm, accs, pr, ysnd, yrcv, run, yb, runt, xt, trcv, tsnd, xb, pcs, psnd, lo,
    lsem, msem, osem,
    u_ss, u_rs, m_ss, m_rs, p_ss, p_rs, y_ss, y_rs, f_ss, f_rs, t_ss, t_rs,
    xd_ss, xd_rs, xu_ss, xu_rs, b_ss, b_rs,
):
    s = lax.axis_index("leaf")
    m = lax.axis_index("sub")
    c = lax.rem(m, 2)
    y = lax.div(m, 2)
    ny = M // 2
    nl = right_h.shape[0]
    SH = srt.shape[0]
    B = SH // WSN
    nbm = SH // BLK
    c1, c2 = nl - 1, nl - 2
    first = {1: 0, 2: c1}
    base = {1: nl, 2: nl + c1}
    width = {1: c1, 2: c2}
    nslots = nl + c1 + c2
    partner = (s, m + 1 - 2 * c)
    up = (s, m + 1)
    down = (s, m - 1)

    def remote(src, dst, ssem, rsem, dev):
        return pltpu.make_async_remote_copy(
            src_ref=src, dst_ref=dst, send_sem=ssem, recv_sem=rsem, device_id=dev, device_id_type=MESH
        )

    locals_in = [
        (right_h, rt, 0), (inv_h, iv, nl), (panels_h, pn, 2 * nl),
    ]
    for j in range(nl):
        for src, dst, at in locals_in:
            pltpu.make_async_copy(src.at[j], dst.at[j], lsem.at[at + j]).start()
    big = [
        pltpu.make_async_copy(sright_h, srt, lsem.at[3 * nl]),
        pltpu.make_async_copy(sinv_h, sinv, lsem.at[3 * nl + 1]),
        pltpu.make_async_copy(fac_h, fac, lsem.at[3 * nl + 2]),
    ]
    for copy in big:
        copy.start()

    barrier = pltpu.get_barrier_semaphore()

    def greet(dev):
        pl.semaphore_signal(barrier, inc=1, device_id=dev, device_id_type=MESH)

    def when_greet(cond, dev):
        pl.when(cond)(lambda: greet(dev))
        return cond.astype(jnp.int32)

    friends = when_greet(m > 0, down) + when_greet(m < M - 1, up)
    for i in range(1, ny):
        greet((s, lax.rem(y + i, ny) * 2 + c))
    for d in (1, 2):
        friends = friends + when_greet(s >= d, (s - d, m))
        friends = friends + when_greet(s + d < S, (s + d, m))

    @pl.loop(0, nl)
    def _(j):
        for src, dst, at in locals_in:
            pltpu.make_async_copy(src.at[j], dst.at[j], lsem.at[at + j]).wait()
        sol = mm(iv[j], rt[j]).astype(BF16)
        ly[j] = sol
        ub[j] = mm(pn[j], sol).astype(BF16)

    def slots(read, sec):
        dist = [sec - read(j, KB) for j in range(nl)]
        rank = []
        for j in range(nl):
            r = jnp.int32(0)
            for i in range(j):
                r = r + (dist[i] == dist[j]).astype(jnp.int32)
            rank.append(r)
        return dist, rank

    own = lambda j, k: tree_s[j] if k == KB else block_s[j, k]
    sub = lax.broadcasted_iota(jnp.int32, mv.shape, 0)
    lane = lax.broadcasted_iota(jnp.int32, mv.shape, 1)
    meta = jnp.zeros(mv.shape, jnp.int32)
    for j in range(nl):
        for k in range(KB + 1):
            meta = jnp.where((sub == j) & (lane == k), own(j, k), meta)
    mv[...] = meta
    dist, rank = slots(own, s)

    pl.semaphore_wait(barrier, friends + (ny - 1))

    def metas(d):
        return remote(mv, mr.at[d - 1], m_ss.at[d - 1], m_rs.at[d - 1], (s - d, m))

    def updates(d, third):
        if third:
            a, b = usnd.at[2], ucat.at[2]
            return remote(a, b, u_ss.at[2], u_rs.at[2], (s - d, m))
        a = usnd.at[pl.ds(first[d], 2)]
        b = ucat.at[pl.ds(first[d], 2)]
        return remote(a, b, u_ss.at[d - 1], u_rs.at[d - 1], (s - d, m))

    for d in (2, 1):
        @pl.when(s >= d)
        def _():
            metas(d).start()
            for q in range(width[d]):
                pick = jnp.int32(0)
                for j in range(nl):
                    pick = jnp.where((dist[j] == d) & (rank[j] == q), j, pick)
                usnd[first[d] + q] = ub[pick]
            updates(d, False).start()
    pl.when(s == 1)(lambda: updates(1, True).start())

    def row_ids(entry):
        lane = lax.broadcasted_iota(jnp.int32, (1, KB * BLK), 1)
        v = jnp.full((1, KB * BLK), entry[KB - 1] * BLK, jnp.int32)
        for k in range(KB - 1):
            v = jnp.where(lane // BLK == k, entry[k] * BLK, v)
        return v + lane % BLK

    def scatter(begin, blocks, pairs, put):
        @pl.loop(0, blocks)
        def _(i):
            at = begin + i * 256
            iota = lax.broadcasted_iota(jnp.int32, (256, KB * BLK), 0) + at
            total = jnp.zeros((256, R), F32)
            for ids, ref, n in pairs:
                pick = jnp.where(iota == ids, 1.0, 0.0).astype(BF16)
                total = total + mm(pick, ref[n])
            put(pl.ds(pl.multiple_of(at, 256), 256), total)

    targets = []
    for j in range(nl):
        targets.append([jnp.where(dist[j] == 0, block_s[j, k], -1) for k in range(KB)])
    pairs = [(row_ids(targets[j]), ub, j) for j in range(nl)]

    def put_own(rows, total):
        accm[rows, :] = total
    scatter(0, SA // 256, pairs, put_own)

    @pl.loop(0, nl)
    def _(j):
        ivt[j] = iv[j].astype(F32).T.astype(BF16)
        pnt[j] = pn[j].astype(F32).T.astype(BF16)

    for d in (1, 2):
        @pl.when(s + d < S)
        def _():
            metas(d).wait_recv()

        @pl.when(s + d >= S)
        def _():
            mr[d - 1] = jnp.full(mr.shape[1:], -1000, jnp.int32)
            ucat[first[d]:first[d] + 2] = jnp.zeros((2, KB * BLK, R), BF16)

        @pl.when(s < d)
        def _():
            pcs[base[d]:base[d] + 2] = jnp.zeros((2, KB * BLK, R), BF16)
        copy = pltpu.make_async_copy(mr.at[d - 1], ms.at[d - 1], msem.at[d - 1])
        copy.start()
        copy.wait()

    @pl.when(s > 0)
    def _():
        ucat[2] = jnp.zeros((KB * BLK, R), BF16)

    @pl.when(s != 1)
    def _():
        pcs[nl + 2] = jnp.zeros((KB * BLK, R), BF16)

    pairs = []
    for d in (1, 2):
        read = lambda j, k, d=d: ms[d - 1, j, k]
        rd, rr = slots(read, s + d)
        for q in range(width[d]):
            entry = []
            for k in range(KB):
                t = jnp.int32(-1)
                for j in range(nl):
                    t = jnp.where((rd[j] == d) & (rr[j] == q), read(j, k), t)
                entry.append(t)
            targets.append(entry)
            pairs.append((row_ids(entry), ucat, first[d] + q))
    third = pairs.pop(2)

    def put_more(rows, total):
        accm[rows, :] += total

    @pl.when(s == 0)
    def _():
        updates(1, True).wait_recv()
        scatter(0, SA // 256, [third], put_more)

    even = lax.rem(s, 2) == 0
    near, far = pairs[:2], pairs[2:]

    def arrived(d):
        pl.when(s + d < S)(lambda: updates(d, False).wait_recv())

    @pl.when(even)
    def _():
        arrived(1)
        scatter(0, SA // 256, near, put_more)
        arrived(2)

    @pl.when(jnp.logical_not(even))
    def _():
        arrived(2)
        scatter(0, SA // 256, far, put_more)
        arrived(1)
    pairs = [
        (jnp.where(even, q[0], p[0]), ucat, jnp.where(even, q[2], p[2])) for p, q in zip(near, far)
    ]

    def pair(o, b):
        return remote(accs.at[o, b], pr.at[o, b], p_ss.at[o, b], p_rs.at[o, b], partner)

    def across(to, frm, b):
        return remote(ysnd.at[to, b], yrcv.at[frm, b], y_ss.at[to, b], y_rs.at[frm, b], (s, to * 2 + c))

    def rows_at(o, core, b):
        return pl.ds(pl.multiple_of((o * 2 + core) * SH + b * WSN, WSN), WSN)

    def more(o, core, b):
        scatter((o * 2 + core) * SH + b * WSN, WSN // 256, pairs, put_more)

    order = [lax.rem(y + i, ny) for i in range(1, ny)] + [y]
    for o in order:
        for b in range(B):
            more(o, 1 - c, b)
            accs[o, b] = accm[rows_at(o, 1 - c, b), :].astype(BF16)
            pair(o, b).start()
            more(o, c, b)
            if o is not y:
                pair(o, b).wait_recv()
                ysnd[o, b] = (accm[rows_at(o, c, b), :] + pr[o, b].astype(F32)).astype(BF16)
                across(o, y, b).start()
    big[0].wait()
    big[1].wait()
    big[2].wait()

    def right_side(b):
        at = pl.ds(b * WSN, WSN)
        pair(y, b).wait_recv()
        side = srt[at, :].astype(F32) - accm[rows_at(y, c, b), :] - pr[y, b].astype(F32)
        for o in order[:-1]:
            across(o, o, b).wait_recv()
            side = side - yrcv[o, b].astype(F32)
        run[at, :] = side.astype(BF16).astype(F32)

    def cols(q):
        return pl.ds(pl.multiple_of(q * WSN, WSN), WSN)

    def forward(q):
        return remote(yb.at[q], yb.at[q], f_ss.at[q], f_rs.at[q], up)

    @pl.when(m > 0)
    def _():
        for b in range(B):
            right_side(b)

    @pl.loop(0, m * B)
    def _(q):
        forward(q).wait_recv()
        pl.when(m < M - 1)(lambda: forward(q).start())
        for b in range(B):
            at = pl.ds(b * WSN, WSN)
            run[at, :] -= mm(fac[at, cols(q)], yb[q])

    for b in range(B):
        at = pl.ds(b * WSN, WSN)
        pl.when(m == 0)(lambda b=b: right_side(b))
        bracket = run[at, :]
        for e in range(b):
            bracket = bracket - mm(fac[at, cols(m * B + e)], yb[m * B + e])
        yb[m * B + b] = mm(sinv[at, :], bracket.astype(BF16)).astype(BF16)
        pl.when(m < M - 1)(lambda b=b: forward(m * B + b).start())
    for b in range(B):
        runt[:, b * WSN:(b + 1) * WSN] = yb[m * B + b].astype(F32).T

    def back(q):
        return remote(tsnd.at[q], trcv.at[q], t_ss.at[q], t_rs.at[q], down)

    nbs = WSN // BLK

    def xdown(q):
        part = xb.at[pl.ds(q * nbs, nbs)]
        return remote(part, part, xd_ss.at[q], xd_rs.at[q], down)

    def xup(q):
        part = xb.at[pl.ds(q * nbs, nbs)]
        return remote(part, part, xu_ss.at[q], xu_rs.at[q], up)

    def turn_x(b):
        block = xt[:, b * WSN:(b + 1) * WSN].astype(F32).T.astype(BF16)
        q = m * B + b
        xb[pl.ds(q * nbs, nbs)] = block.reshape(nbs, BLK, R)

    def send_x(b):
        q = m * B + b
        pl.when(m < M - 1)(lambda: xup(q).start())
        pl.when(m > 0)(lambda: xdown(q).start())

    for b in reversed(range(B)):
        at = pl.ds(b * WSN, WSN)

        @pl.when(m < M - 1)
        def _():
            back(m * B + b).wait_recv()
            runt[:, at] -= trcv[m * B + b].astype(F32)
        bracket = runt[:, at]
        for e in range(b + 1, B):
            rows = pl.ds(e * WSN, WSN)
            bracket = bracket - mm(xt[:, rows], fac[rows, cols(m * B + b)])
        xt[:, at] = mm(bracket.astype(BF16), sinv[at, :]).astype(BF16)

        @pl.when(m == 0)
        def _():
            turn_x(b)
            send_x(b)

    @pl.loop(0, m * B)
    def _(i):
        q = m * B - 1 - i
        pl.when(m < M - 1)(lambda: back(q).wait_recv())
        term = mm(xt[...], fac[:, cols(q)])
        before = jnp.where(m < M - 1, trcv[q].astype(F32), 0.0)
        tsnd[q] = (term + before).astype(BF16)
        back(q).start()

    @pl.when(m > 0)
    def _():
        for b in reversed(range(B)):
            turn_x(b)

        @pl.loop(0, m * B)
        def _(q):
            back(q).wait_send()
        for b in reversed(range(B)):
            send_x(b)

    out_sep = pltpu.make_async_copy(xb.at[pl.ds(m * nbm, nbm)], osx, osem.at[nl])
    out_sep.start()

    @pl.loop(0, (M - 1 - m) * B)
    def _(i):
        q = M * B - 1 - i
        xdown(q).wait_recv()
        pl.when(m > 0)(lambda: xdown(q).start())

    @pl.loop(0, m * B)
    def _(i):
        q = m * B - 1 - i
        xup(q).wait_recv()
        pl.when(m < M - 1)(lambda: xup(q).start())

    def pieces(d, third):
        if third:
            return remote(psnd.at[2], pcs.at[nl + 2], b_ss.at[2], b_rs.at[2], (s + d, m))
        a = psnd.at[pl.ds(first[d], 2)]
        b = pcs.at[pl.ds(base[d], 2)]
        return remote(a, b, b_ss.at[d - 1], b_rs.at[d - 1], (s + d, m))

    for d in (2, 1):
        @pl.when(s + d < S)
        def _():
            for q in range(width[d]):
                for k in range(KB):
                    t = jnp.maximum(targets[base[d] + q][k], 0)
                    psnd[first[d] + q, k * BLK:(k + 1) * BLK, :] = xb[t]
            pieces(d, False).start()
    pl.when(s == 0)(lambda: pieces(1, True).start())
    for j in range(nl):
        for k in range(KB):
            pcs[j, k * BLK:(k + 1) * BLK, :] = xb[block_s[j, k]]
    for d in (1, 2):
        pl.when(s >= d)(lambda d=d: pieces(d, False).wait_recv())
    pl.when(s == 1)(lambda: pieces(1, True).wait_recv())

    for j in range(nl):
        at = jnp.where(dist[j] == 0, j, jnp.where(dist[j] == 1, nl + rank[j], nl + c1 + rank[j]))
        at = jnp.clip(at, 0, nslots - 1)
        reduced = mm(pnt[j], pcs[at])
        inner = (ly[j].astype(F32) - reduced).astype(BF16)
        lo[j] = mm(ivt[j], inner).astype(BF16)
        pltpu.make_async_copy(lo.at[j], ox.at[j], osem.at[j]).start()

    for d in (1, 2):
        @pl.when(s >= d)
        def _():
            metas(d).wait_send()
            updates(d, False).wait_send()

        pl.when(s + d < S)(lambda d=d: pieces(d, False).wait_send())
    pl.when(s == 1)(lambda: updates(1, True).wait_send())
    pl.when(s == 0)(lambda: pieces(1, True).wait_send())
    for o in order:
        for b in range(B):
            pair(o, b).wait_send()
            if o is not y:
                across(o, y, b).wait_send()

    @pl.when(m < M - 1)
    def _():
        @pl.loop(0, (m + 1) * B)
        def _(q):
            forward(q).wait_send()
            xup(q).wait_send()

    @pl.when(m > 0)
    def _():
        @pl.loop(m * B, M * B)
        def _(q):
            xdown(q).wait_send()

    out_sep.wait()
    for j in range(nl):
        pltpu.make_async_copy(lo.at[j], ox.at[j], osem.at[j]).wait()


def shards(S, M, leaf_right, leaf_inverse, panels, leaf_subtree, panel_block, separator_right, separator_inverse, separator_factor):
    nl, W = leaf_right.shape[:2]
    SH = separator_right.shape[0]
    ny = M // 2
    nbm = SH // BLK
    B = SH // WSN
    N = SA // WSN
    nslots = 3 * nl - 3
    anywhere = pl.BlockSpec(memory_space=pl.ANY)
    V = pltpu.VMEM
    D = pltpu.SemaphoreType.DMA
    scratch = [
        V((nl, W, R), BF16), V((nl, W, W), BF16), V((nl, KB * BLK, W), BF16),
        V((SH, R), BF16), V((SH, WSN), BF16), V((SH, SA), BF16),
        V((nl, W, W), BF16), V((nl, W, KB * BLK), BF16),
        V((nl, W, R), BF16), V((nl, KB * BLK, R), BF16), V((2 * nl - 3, KB * BLK, R), BF16), V((2 * nl - 3, KB * BLK, R), BF16),
        V((8, 128), jnp.int32), V((2, 8, 128), jnp.int32), pltpu.SMEM((2, 8, 128), jnp.int32),
        V((SA, R), F32), V((ny, B, WSN, R), BF16), V((ny, B, WSN, R), BF16), V((ny, B, WSN, R), BF16), V((ny, B, WSN, R), BF16),
        V((SH, R), F32), V((N, WSN, R), BF16), V((R, SH), F32), V((R, SH), BF16),
        V((N, R, WSN), BF16), V((N, R, WSN), BF16), V((SA // BLK, BLK, R), BF16),
        V((nslots, KB * BLK, R), BF16), V((2 * nl - 3, KB * BLK, R), BF16), V((nl, W, R), BF16),
        D((3 * nl + 3,)), D((2,)), D((nl + 1,)),
        D((3,)), D((3,)), D((2,)), D((2,)), D((ny, B)), D((ny, B)), D((ny, B)), D((ny, B)),
        D((N,)), D((N,)), D((N,)), D((N,)), D((N,)), D((N,)), D((N,)), D((N,)), D((3,)), D((3,)),
    ]
    leaf_x, sep_x = pl.pallas_call(
        functools.partial(kernel, S, M),
        out_shape=(
            jax.ShapeDtypeStruct((nl, W, R), BF16),
            jax.ShapeDtypeStruct((nbm, BLK, R), BF16),
        ),
        in_specs=[
            anywhere, anywhere, anywhere,
            pl.BlockSpec(memory_space=pltpu.SMEM), pl.BlockSpec(memory_space=pltpu.SMEM),
            anywhere, anywhere, anywhere,
        ],
        out_specs=(anywhere, anywhere),
        scratch_shapes=scratch,
        compiler_params=pltpu.CompilerParams(
            collective_id=0, has_side_effects=True, vmem_limit_bytes=56 * 1024 * 1024
        ),
        cost_estimate=pl.CostEstimate(flops=12_000_000_000, bytes_accessed=16_000_000, transcendentals=0),
    )(leaf_right, leaf_inverse, panels, panel_block, leaf_subtree, separator_right, separator_inverse, separator_factor)
    return leaf_x, sep_x.reshape(SH, R)


def solution(mesh):
    placed = (
        P(("leaf", "sub"), None, None),
        P(("leaf", "sub"), None, None),
        P(("leaf", "sub"), None, None),
        P(("leaf", "sub")),
        P(("leaf", "sub"), None),
        P(("leaf", "sub"), None),
        P(("leaf", "sub"), None),
        P(("leaf", "sub"), None),
    )
    return jax.shard_map(
        functools.partial(shards, mesh.shape["leaf"], mesh.shape["sub"]),
        mesh=mesh,
        in_specs=placed,
        out_specs=(P(("leaf", "sub"), None, None), P(("leaf", "sub"), None)),
        check_vma=False,
    )
```

```python
import functools

import jax
import jax.numpy as jnp
from jax import lax
from jax.experimental import pallas as pl
from jax.experimental.pallas import tpu as pltpu
from jax.sharding import PartitionSpec as P

WSN = 512
SA = 4096
R = 256
BLK = 64
KB = 4
SPAN = 3
MESH = pl.DeviceIdType.MESH
F32 = jnp.float32
BF16 = jnp.bfloat16


def mm(a, b):
    return jnp.dot(a, b, preferred_element_type=F32)


def mm_t(a, b):
    return lax.dot_general(a, b, (((0,), (0,)), ((), ())), preferred_element_type=F32)


def kernel(
    S, M,
    right_h, inv_h, panels_h, block_s, tree_s, sright_h, sinv_h, fac_h,
    ox, osx,
    rt, iv, pn, srt, sinv, fac,
    ivt, pnt, ly, ub, ucat, usnd, mv, mr, ms,
    accm, accs, pr, ysnd, yrcv, run, yb, runt, xt, trcv, tsnd, xb, pcs, psnd, lo,
    lsem, msem, osem,
    u_ss, u_rs, m_ss, m_rs, p_ss, p_rs, y_ss, y_rs, f_ss, f_rs, t_ss, t_rs,
    xd_ss, xd_rs, xu_ss, xu_rs, b_ss, b_rs,
):
    s = lax.axis_index("leaf")
    m = lax.axis_index("sub")
    c = lax.rem(m, 2)
    y = lax.div(m, 2)
    ny = M // 2
    nl = right_h.shape[0]
    SH = srt.shape[0]
    B = SH // WSN
    nbm = SH // BLK
    c1, c2 = nl - 1, nl - 2
    first = {1: 0, 2: c1}
    base = {1: nl, 2: nl + c1}
    width = {1: c1, 2: c2}
    nslots = nl + c1 + c2
    partner = (s, m + 1 - 2 * c)
    up = (s, m + 1)
    down = (s, m - 1)

    def remote(src, dst, ssem, rsem, dev):
        return pltpu.make_async_remote_copy(
            src_ref=src, dst_ref=dst, send_sem=ssem, recv_sem=rsem, device_id=dev, device_id_type=MESH
        )

    locals_in = [
        (right_h, rt, 0), (inv_h, iv, nl), (panels_h, pn, 2 * nl),
    ]
    for j in range(nl):
        for src, dst, at in locals_in:
            pltpu.make_async_copy(src.at[j], dst.at[j], lsem.at[at + j]).start()
    big = [
        pltpu.make_async_copy(sright_h, srt, lsem.at[3 * nl]),
        pltpu.make_async_copy(sinv_h, sinv, lsem.at[3 * nl + 1]),
        pltpu.make_async_copy(fac_h, fac, lsem.at[3 * nl + 2]),
    ]
    for copy in big:
        copy.start()

    barrier = pltpu.get_barrier_semaphore()

    def greet(dev):
        pl.semaphore_signal(barrier, inc=1, device_id=dev, device_id_type=MESH)

    def when_greet(cond, dev):
        pl.when(cond)(lambda: greet(dev))
        return cond.astype(jnp.int32)

    friends = jnp.int32(M - 1)
    for i in range(1, M):
        greet((s, lax.rem(m + i, M)))
    for d in (1, 2):
        friends = friends + when_greet(s >= d, (s - d, m))
        friends = friends + when_greet(s + d < S, (s + d, m))

    @pl.loop(0, nl)
    def _(j):
        for src, dst, at in locals_in:
            pltpu.make_async_copy(src.at[j], dst.at[j], lsem.at[at + j]).wait()
        sol = mm(iv[j], rt[j]).astype(BF16)
        ly[j] = sol
        ub[j] = mm(pn[j], sol).astype(BF16)

    def slots(read, sec):
        dist = [sec - read(j, KB) for j in range(nl)]
        rank = []
        for j in range(nl):
            r = jnp.int32(0)
            for i in range(j):
                r = r + (dist[i] == dist[j]).astype(jnp.int32)
            rank.append(r)
        return dist, rank

    own = lambda j, k: tree_s[j] if k == KB else block_s[j, k]
    sub = lax.broadcasted_iota(jnp.int32, mv.shape, 0)
    lane = lax.broadcasted_iota(jnp.int32, mv.shape, 1)
    meta = jnp.zeros(mv.shape, jnp.int32)
    for j in range(nl):
        for k in range(KB + 1):
            meta = jnp.where((sub == j) & (lane == k), own(j, k), meta)
    mv[...] = meta
    dist, rank = slots(own, s)

    pl.semaphore_wait(barrier, friends)

    def metas(d):
        return remote(mv, mr.at[d - 1], m_ss.at[d - 1], m_rs.at[d - 1], (s - d, m))

    def updates(d, third):
        if third:
            a, b = usnd.at[2], ucat.at[2]
            return remote(a, b, u_ss.at[2], u_rs.at[2], (s - d, m))
        a = usnd.at[pl.ds(first[d], 2)]
        b = ucat.at[pl.ds(first[d], 2)]
        return remote(a, b, u_ss.at[d - 1], u_rs.at[d - 1], (s - d, m))

    for d in (2, 1):
        @pl.when(s >= d)
        def _():
            metas(d).start()
            for q in range(width[d]):
                pick = jnp.int32(0)
                for j in range(nl):
                    pick = jnp.where((dist[j] == d) & (rank[j] == q), j, pick)
                usnd[first[d] + q] = ub[pick]
            updates(d, False).start()
    pl.when(s == 1)(lambda: updates(1, True).start())

    def row_ids(entry):
        lane = lax.broadcasted_iota(jnp.int32, (1, KB * BLK), 1)
        v = jnp.full((1, KB * BLK), entry[KB - 1] * BLK, jnp.int32)
        for k in range(KB - 1):
            v = jnp.where(lane // BLK == k, entry[k] * BLK, v)
        return v + lane % BLK

    def scatter(begin, blocks, pairs, put):
        @pl.loop(0, blocks)
        def _(i):
            at = begin + i * 256
            iota = lax.broadcasted_iota(jnp.int32, (256, KB * BLK), 0) + at
            total = jnp.zeros((256, R), F32)
            for ids, ref, n in pairs:
                pick = jnp.where(iota == ids, 1.0, 0.0).astype(BF16)
                total = total + mm(pick, ref[n])
            put(pl.ds(pl.multiple_of(at, 256), 256), total)

    targets = []
    for j in range(nl):
        targets.append([jnp.where(dist[j] == 0, block_s[j, k], -1) for k in range(KB)])
    pairs = [(row_ids(targets[j]), ub, j) for j in range(nl)]

    def put_own(rows, total):
        accm[rows, :] = total
    scatter(0, SA // 256, pairs, put_own)

    @pl.loop(0, nl)
    def _(j):
        ivt[j] = iv[j].astype(F32).T.astype(BF16)
        pnt[j] = pn[j].astype(F32).T.astype(BF16)

    for d in (1, 2):
        @pl.when(s + d < S)
        def _():
            metas(d).wait_recv()

        @pl.when(s + d >= S)
        def _():
            mr[d - 1] = jnp.full(mr.shape[1:], -1000, jnp.int32)
            ucat[first[d]:first[d] + 2] = jnp.zeros((2, KB * BLK, R), BF16)

        @pl.when(s < d)
        def _():
            pcs[base[d]:base[d] + 2] = jnp.zeros((2, KB * BLK, R), BF16)
        copy = pltpu.make_async_copy(mr.at[d - 1], ms.at[d - 1], msem.at[d - 1])
        copy.start()
        copy.wait()

    @pl.when(s > 0)
    def _():
        ucat[2] = jnp.zeros((KB * BLK, R), BF16)

    @pl.when(s != 1)
    def _():
        pcs[nl + 2] = jnp.zeros((KB * BLK, R), BF16)

    pairs = []
    for d in (1, 2):
        read = lambda j, k, d=d: ms[d - 1, j, k]
        rd, rr = slots(read, s + d)
        for q in range(width[d]):
            entry = []
            for k in range(KB):
                t = jnp.int32(-1)
                for j in range(nl):
                    t = jnp.where((rd[j] == d) & (rr[j] == q), read(j, k), t)
                entry.append(t)
            targets.append(entry)
            pairs.append((row_ids(entry), ucat, first[d] + q))
    third = pairs.pop(2)

    def put_more(rows, total):
        accm[rows, :] += total

    @pl.when(s == 0)
    def _():
        updates(1, True).wait_recv()
        scatter(0, SA // 256, [third], put_more)

    even = lax.rem(s, 2) == 0
    near, far = pairs[:2], pairs[2:]

    def arrived(d):
        pl.when(s + d < S)(lambda: updates(d, False).wait_recv())

    @pl.when(even)
    def _():
        arrived(1)
        scatter(0, SA // 256, near, put_more)
        arrived(2)

    @pl.when(jnp.logical_not(even))
    def _():
        arrived(2)
        scatter(0, SA // 256, far, put_more)
        arrived(1)
    pairs = [
        (jnp.where(even, q[0], p[0]), ucat, jnp.where(even, q[2], p[2])) for p, q in zip(near, far)
    ]

    def pair(o, b):
        return remote(accs.at[o, b], pr.at[o, b], p_ss.at[o, b], p_rs.at[o, b], partner)

    def across(to, frm, b):
        return remote(ysnd.at[to, b], yrcv.at[frm, b], y_ss.at[to, b], y_rs.at[frm, b], (s, to * 2 + c))

    def rows_at(o, core, b):
        return pl.ds(pl.multiple_of((o * 2 + core) * SH + b * WSN, WSN), WSN)

    def more(o, core, b):
        scatter((o * 2 + core) * SH + b * WSN, WSN // 256, pairs, put_more)

    order = [lax.rem(y + i, ny) for i in range(1, ny)] + [y]
    for o in order:
        for b in range(B):
            more(o, 1 - c, b)
            accs[o, b] = accm[rows_at(o, 1 - c, b), :].astype(BF16)
            pair(o, b).start()
            more(o, c, b)
            if o is not y:
                pair(o, b).wait_recv()
                ysnd[o, b] = (accm[rows_at(o, c, b), :] + pr[o, b].astype(F32)).astype(BF16)
                across(o, y, b).start()
    big[0].wait()
    big[1].wait()
    big[2].wait()

    def right_side(b):
        at = pl.ds(b * WSN, WSN)
        pair(y, b).wait_recv()
        side = srt[at, :].astype(F32) - accm[rows_at(y, c, b), :] - pr[y, b].astype(F32)
        for o in order[:-1]:
            across(o, o, b).wait_recv()
            side = side - yrcv[o, b].astype(F32)
        run[at, :] = side.astype(BF16).astype(F32)

    def cols(q):
        return pl.ds(pl.multiple_of(q * WSN, WSN), WSN)

    def forward(q):
        return remote(yb.at[q], yb.at[q], f_ss.at[q], f_rs.at[q], up)

    @pl.when(m > 0)
    def _():
        for b in range(B):
            right_side(b)

    @pl.loop(0, m * B)
    def _(q):
        forward(q).wait_recv()
        pl.when(m < M - 1)(lambda: forward(q).start())
        for b in range(B):
            at = pl.ds(b * WSN, WSN)
            run[at, :] -= mm(fac[at, cols(q)], yb[q])

    for b in range(B):
        at = pl.ds(b * WSN, WSN)
        pl.when(m == 0)(lambda b=b: right_side(b))
        bracket = run[at, :]
        for e in range(b):
            bracket = bracket - mm(fac[at, cols(m * B + e)], yb[m * B + e])
        yb[m * B + b] = mm(sinv[at, :], bracket.astype(BF16)).astype(BF16)
        pl.when(m < M - 1)(lambda b=b: forward(m * B + b).start())
    for b in range(B):
        runt[:, b * WSN:(b + 1) * WSN] = yb[m * B + b].astype(F32).T

    def back(q):
        return remote(tsnd.at[q], trcv.at[q], t_ss.at[q], t_rs.at[q], down)

    nbs = WSN // BLK

    def xdown(q):
        part = xb.at[pl.ds(q * nbs, nbs)]
        return remote(part, part, xd_ss.at[q], xd_rs.at[q], down)

    def xup(q, to):
        part = xb.at[pl.ds(q * nbs, nbs)]
        return remote(part, part, xu_ss.at[q, to], xu_rs.at[q], (s, to))

    def later_chips(act):
        for o in range(1, ny):
            pl.when(o > y)(lambda o=o: act(2 * o))

    def turn_x(b):
        block = xt[:, b * WSN:(b + 1) * WSN].astype(F32).T.astype(BF16)
        q = m * B + b
        xb[pl.ds(q * nbs, nbs)] = block.reshape(nbs, BLK, R)

    def send_x(b):
        q = m * B + b
        later_chips(lambda to: xup(q, to).start())
        pl.when(c == 0)(lambda: xup(q, m + 1).start())
        pl.when(m > 0)(lambda: xdown(q).start())

    for b in reversed(range(B)):
        at = pl.ds(b * WSN, WSN)

        @pl.when(m < M - 1)
        def _():
            back(m * B + b).wait_recv()
            runt[:, at] -= trcv[m * B + b].astype(F32)
        bracket = runt[:, at]
        for e in range(b + 1, B):
            rows = pl.ds(e * WSN, WSN)
            bracket = bracket - mm(xt[:, rows], fac[rows, cols(m * B + b)])
        xt[:, at] = mm(bracket.astype(BF16), sinv[at, :]).astype(BF16)

        @pl.when(m == 0)
        def _():
            turn_x(b)
            send_x(b)

    @pl.loop(0, m * B)
    def _(i):
        q = m * B - 1 - i
        pl.when(m < M - 1)(lambda: back(q).wait_recv())
        term = mm(xt[...], fac[:, cols(q)])
        before = jnp.where(m < M - 1, trcv[q].astype(F32), 0.0)
        tsnd[q] = (term + before).astype(BF16)
        back(q).start()

    @pl.when(m > 0)
    def _():
        for b in reversed(range(B)):
            turn_x(b)

        @pl.loop(0, m * B)
        def _(q):
            back(q).wait_send()
        for b in reversed(range(B)):
            send_x(b)

    out_sep = pltpu.make_async_copy(xb.at[pl.ds(m * nbm, nbm)], osx, osem.at[nl])
    out_sep.start()

    @pl.loop(0, (M - 1 - m) * B)
    def _(i):
        q = M * B - 1 - i
        xdown(q).wait_recv()
        pl.when(m > 0)(lambda: xdown(q).start())

    @pl.loop(0, m * B)
    def _(i):
        q = m * B - 1 - i
        xup(q, m).wait_recv()
        pl.when(c == 0)(lambda: xup(q, m + 1).start())

    def pieces(d, third):
        if third:
            return remote(psnd.at[2], pcs.at[nl + 2], b_ss.at[2], b_rs.at[2], (s + d, m))
        a = psnd.at[pl.ds(first[d], 2)]
        b = pcs.at[pl.ds(base[d], 2)]
        return remote(a, b, b_ss.at[d - 1], b_rs.at[d - 1], (s + d, m))

    for d in (2, 1):
        @pl.when(s + d < S)
        def _():
            for q in range(width[d]):
                for k in range(KB):
                    t = jnp.maximum(targets[base[d] + q][k], 0)
                    psnd[first[d] + q, k * BLK:(k + 1) * BLK, :] = xb[t]
            pieces(d, False).start()
    pl.when(s == 0)(lambda: pieces(1, True).start())
    for j in range(nl):
        for k in range(KB):
            pcs[j, k * BLK:(k + 1) * BLK, :] = xb[block_s[j, k]]
    for d in (1, 2):
        pl.when(s >= d)(lambda d=d: pieces(d, False).wait_recv())
    pl.when(s == 1)(lambda: pieces(1, True).wait_recv())

    for j in range(nl):
        at = jnp.where(dist[j] == 0, j, jnp.where(dist[j] == 1, nl + rank[j], nl + c1 + rank[j]))
        at = jnp.clip(at, 0, nslots - 1)
        reduced = mm(pnt[j], pcs[at])
        inner = (ly[j].astype(F32) - reduced).astype(BF16)
        lo[j] = mm(ivt[j], inner).astype(BF16)
        pltpu.make_async_copy(lo.at[j], ox.at[j], osem.at[j]).start()

    for d in (1, 2):
        @pl.when(s >= d)
        def _():
            metas(d).wait_send()
            updates(d, False).wait_send()

        pl.when(s + d < S)(lambda d=d: pieces(d, False).wait_send())
    pl.when(s == 1)(lambda: updates(1, True).wait_send())
    pl.when(s == 0)(lambda: pieces(1, True).wait_send())
    for o in order:
        for b in range(B):
            pair(o, b).wait_send()
            if o is not y:
                across(o, y, b).wait_send()

    @pl.when(m < M - 1)
    def _():
        @pl.loop(0, (m + 1) * B)
        def _(q):
            forward(q).wait_send()

    @pl.when(c == 0)
    def _():
        @pl.loop(0, (m + 1) * B)
        def _(q):
            xup(q, m + 1).wait_send()

    for b in range(B):
        later_chips(lambda to, b=b: xup(m * B + b, to).wait_send())

    @pl.when(m > 0)
    def _():
        @pl.loop(m * B, M * B)
        def _(q):
            xdown(q).wait_send()

    out_sep.wait()
    for j in range(nl):
        pltpu.make_async_copy(lo.at[j], ox.at[j], osem.at[j]).wait()


def write_out(leaf_h, sep_h, ox, osx, sem):
    nl = leaf_h.shape[0]
    half = sep_h.shape[0] // 2
    copies = [pltpu.make_async_copy(leaf_h.at[j], ox.at[j], sem.at[j]) for j in range(nl)]
    for i in range(2):
        part = pl.ds(i * half, half)
        copies.append(pltpu.make_async_copy(sep_h.at[part], osx.at[part], sem.at[nl + i]))
    for copy in copies:
        copy.start()
    for copy in copies:
        copy.wait()


def shards(S, M, leaf_right, leaf_inverse, panels, leaf_subtree, panel_block, separator_right, separator_inverse, separator_factor):
    nl, W = leaf_right.shape[:2]
    SH = separator_right.shape[0]
    ny = M // 2
    nbm = SH // BLK
    B = SH // WSN
    N = SA // WSN
    nslots = 3 * nl - 3
    anywhere = pl.BlockSpec(memory_space=pl.ANY)
    V = pltpu.VMEM
    D = pltpu.SemaphoreType.DMA
    scratch = [
        V((nl, W, R), BF16), V((nl, W, W), BF16), V((nl, KB * BLK, W), BF16),
        V((SH, R), BF16), V((SH, WSN), BF16), V((SH, SA), BF16),
        V((nl, W, W), BF16), V((nl, W, KB * BLK), BF16),
        V((nl, W, R), BF16), V((nl, KB * BLK, R), BF16), V((2 * nl - 3, KB * BLK, R), BF16), V((2 * nl - 3, KB * BLK, R), BF16),
        V((8, 128), jnp.int32), V((2, 8, 128), jnp.int32), pltpu.SMEM((2, 8, 128), jnp.int32),
        V((SA, R), F32), V((ny, B, WSN, R), BF16), V((ny, B, WSN, R), BF16), V((ny, B, WSN, R), BF16), V((ny, B, WSN, R), BF16),
        V((SH, R), F32), V((N, WSN, R), BF16), V((R, SH), F32), V((R, SH), BF16),
        V((N, R, WSN), BF16), V((N, R, WSN), BF16), V((SA // BLK, BLK, R), BF16),
        V((nslots, KB * BLK, R), BF16), V((2 * nl - 3, KB * BLK, R), BF16), V((nl, W, R), BF16),
        D((3 * nl + 3,)), D((2,)), D((nl + 1,)),
        D((3,)), D((3,)), D((2,)), D((2,)), D((ny, B)), D((ny, B)), D((ny, B)), D((ny, B)),
        D((N,)), D((N,)), D((N,)), D((N,)), D((N,)), D((N,)), D((N, M)), D((N,)), D((3,)), D((3,)),
    ]
    leaf_x, sep_x = pl.pallas_call(
        functools.partial(kernel, S, M),
        out_shape=(
            jax.ShapeDtypeStruct((nl, W, R), BF16),
            jax.ShapeDtypeStruct((nbm, BLK, R), BF16),
        ),
        in_specs=[
            anywhere, anywhere, anywhere,
            pl.BlockSpec(memory_space=pltpu.SMEM), pl.BlockSpec(memory_space=pltpu.SMEM),
            anywhere, anywhere, anywhere,
        ],
        out_specs=(anywhere, anywhere),
        scratch_shapes=scratch,
        compiler_params=pltpu.CompilerParams(
            collective_id=0, has_side_effects=True, vmem_limit_bytes=56 * 1024 * 1024
        ),
        cost_estimate=pl.CostEstimate(flops=12_000_000_000, bytes_accessed=16_000_000, transcendentals=0),
    )(leaf_right, leaf_inverse, panels, panel_block, leaf_subtree, separator_right, separator_inverse, separator_factor)
    leaf_x, sep_x = pl.pallas_call(
        write_out,
        out_shape=(
            jax.ShapeDtypeStruct((nl, W, R), BF16),
            jax.ShapeDtypeStruct((nbm, BLK, R), BF16),
        ),
        in_specs=[anywhere, anywhere],
        out_specs=(anywhere, anywhere),
        scratch_shapes=[D((nl + 2,))],
        cost_estimate=pl.CostEstimate(flops=0, bytes_accessed=3_000_000, transcendentals=0),
    )(leaf_x, sep_x)
    return leaf_x, sep_x.reshape(SH, R)


def solution(mesh):
    placed = (
        P(("leaf", "sub"), None, None),
        P(("leaf", "sub"), None, None),
        P(("leaf", "sub"), None, None),
        P(("leaf", "sub")),
        P(("leaf", "sub"), None),
        P(("leaf", "sub"), None),
        P(("leaf", "sub"), None),
        P(("leaf", "sub"), None),
    )
    return jax.shard_map(
        functools.partial(shards, mesh.shape["leaf"], mesh.shape["sub"]),
        mesh=mesh,
        in_specs=placed,
        out_specs=(P(("leaf", "sub"), None, None), P(("leaf", "sub"), None)),
        check_vma=False,
    )
```

```python
import functools

import jax
import jax.numpy as jnp
from jax import lax
from jax.experimental import pallas as pl
from jax.experimental.pallas import tpu as pltpu
from jax.sharding import PartitionSpec as P

WSN = 512
SA = 4096
R = 256
BLK = 64
KB = 4
SPAN = 3
MESH = pl.DeviceIdType.MESH
F32 = jnp.float32
BF16 = jnp.bfloat16


def mm(a, b):
    return jnp.dot(a, b, preferred_element_type=F32)


def mm_t(a, b):
    return lax.dot_general(a, b, (((0,), (0,)), ((), ())), preferred_element_type=F32)


def kernel(
    S, M,
    right_h, inv_h, panels_h, block_s, tree_s, sright_h, sinv_h, fac_h,
    ox, osx,
    rt, iv, pn, srt, sinv, fac,
    ivt, pnt, ly, ub, ucat, usnd, mv, mr, ms,
    accm, accs, pr, ysnd, yrcv, run, yb, runt, xt, trcv, tsnd, xb, pcs, psnd, lo,
    lsem, msem, osem,
    u_ss, u_rs, m_ss, m_rs, p_ss, p_rs, y_ss, y_rs, f_ss, f_rs, t_ss, t_rs,
    xd_ss, xd_rs, xu_ss, xu_rs, b_ss, b_rs,
):
    s = lax.axis_index("leaf")
    m = lax.axis_index("sub")
    c = lax.rem(m, 2)
    y = lax.div(m, 2)
    ny = M // 2
    nl = right_h.shape[0]
    SH = srt.shape[0]
    B = SH // WSN
    nbm = SH // BLK
    c1, c2 = nl - 1, nl - 2
    first = {1: 0, 2: c1}
    base = {1: nl, 2: nl + c1}
    width = {1: c1, 2: c2}
    nslots = nl + c1 + c2
    partner = (s, m + 1 - 2 * c)
    up = (s, m + 1)
    down = (s, m - 1)

    def remote(src, dst, ssem, rsem, dev):
        return pltpu.make_async_remote_copy(
            src_ref=src, dst_ref=dst, send_sem=ssem, recv_sem=rsem, device_id=dev, device_id_type=MESH
        )

    locals_in = [
        (right_h, rt, 0), (inv_h, iv, nl), (panels_h, pn, 2 * nl),
    ]
    for j in range(nl):
        for src, dst, at in locals_in:
            pltpu.make_async_copy(src.at[j], dst.at[j], lsem.at[at + j]).start()
    big = [
        pltpu.make_async_copy(sright_h, srt, lsem.at[3 * nl]),
        pltpu.make_async_copy(sinv_h, sinv, lsem.at[3 * nl + 1]),
        pltpu.make_async_copy(fac_h, fac, lsem.at[3 * nl + 2]),
    ]
    for copy in big:
        copy.start()

    barrier = pltpu.get_barrier_semaphore()

    def greet(dev):
        pl.semaphore_signal(barrier, inc=1, device_id=dev, device_id_type=MESH)

    def when_greet(cond, dev):
        pl.when(cond)(lambda: greet(dev))
        return cond.astype(jnp.int32)

    friends = jnp.int32(M - 1)
    for i in range(1, M):
        greet((s, lax.rem(m + i, M)))
    for d in (1, 2):
        friends = friends + when_greet(s >= d, (s - d, m))
        friends = friends + when_greet(s + d < S, (s + d, m))

    @pl.loop(0, nl)
    def _(j):
        for src, dst, at in locals_in:
            pltpu.make_async_copy(src.at[j], dst.at[j], lsem.at[at + j]).wait()
        sol = mm(iv[j], rt[j]).astype(BF16)
        ly[j] = sol
        ub[j] = mm(pn[j], sol).astype(BF16)

    def slots(read, sec):
        dist = [sec - read(j, KB) for j in range(nl)]
        rank = []
        for j in range(nl):
            r = jnp.int32(0)
            for i in range(j):
                r = r + (dist[i] == dist[j]).astype(jnp.int32)
            rank.append(r)
        return dist, rank

    own = lambda j, k: tree_s[j] if k == KB else block_s[j, k]
    sub = lax.broadcasted_iota(jnp.int32, mv.shape, 0)
    lane = lax.broadcasted_iota(jnp.int32, mv.shape, 1)
    meta = jnp.zeros(mv.shape, jnp.int32)
    for j in range(nl):
        for k in range(KB + 1):
            meta = jnp.where((sub == j) & (lane == k), own(j, k), meta)
    mv[...] = meta
    dist, rank = slots(own, s)

    pl.semaphore_wait(barrier, friends)

    def metas(d):
        return remote(mv, mr.at[d - 1], m_ss.at[d - 1], m_rs.at[d - 1], (s - d, m))

    def updates(d, third):
        if third:
            a, b = usnd.at[2], ucat.at[2]
            return remote(a, b, u_ss.at[2], u_rs.at[2], (s - d, m))
        a = usnd.at[pl.ds(first[d], 2)]
        b = ucat.at[pl.ds(first[d], 2)]
        return remote(a, b, u_ss.at[d - 1], u_rs.at[d - 1], (s - d, m))

    for d in (2, 1):
        @pl.when(s >= d)
        def _():
            metas(d).start()
            for q in range(width[d]):
                pick = jnp.int32(0)
                for j in range(nl):
                    pick = jnp.where((dist[j] == d) & (rank[j] == q), j, pick)
                usnd[first[d] + q] = ub[pick]
            updates(d, False).start()
    pl.when(s == 1)(lambda: updates(1, True).start())

    def row_ids(entry):
        lane = lax.broadcasted_iota(jnp.int32, (1, KB * BLK), 1)
        v = jnp.full((1, KB * BLK), entry[KB - 1] * BLK, jnp.int32)
        for k in range(KB - 1):
            v = jnp.where(lane // BLK == k, entry[k] * BLK, v)
        return v + lane % BLK

    def scatter(begin, blocks, pairs, put):
        @pl.loop(0, blocks)
        def _(i):
            at = begin + i * 256
            iota = lax.broadcasted_iota(jnp.int32, (256, KB * BLK), 0) + at
            total = jnp.zeros((256, R), F32)
            for ids, ref, n in pairs:
                pick = jnp.where(iota == ids, 1.0, 0.0).astype(BF16)
                total = total + mm(pick, ref[n])
            put(pl.ds(pl.multiple_of(at, 256), 256), total)

    targets = []
    for j in range(nl):
        targets.append([jnp.where(dist[j] == 0, block_s[j, k], -1) for k in range(KB)])
    pairs = [(row_ids(targets[j]), ub, j) for j in range(nl)]

    def put_own(rows, total):
        accm[rows, :] = total
    scatter(0, SA // 256, pairs, put_own)

    @pl.loop(0, nl)
    def _(j):
        ivt[j] = iv[j].astype(F32).T.astype(BF16)
        pnt[j] = pn[j].astype(F32).T.astype(BF16)

    for d in (1, 2):
        @pl.when(s + d < S)
        def _():
            metas(d).wait_recv()

        @pl.when(s + d >= S)
        def _():
            mr[d - 1] = jnp.full(mr.shape[1:], -1000, jnp.int32)
            ucat[first[d]:first[d] + 2] = jnp.zeros((2, KB * BLK, R), BF16)

        @pl.when(s < d)
        def _():
            pcs[base[d]:base[d] + 2] = jnp.zeros((2, KB * BLK, R), BF16)
        copy = pltpu.make_async_copy(mr.at[d - 1], ms.at[d - 1], msem.at[d - 1])
        copy.start()
        copy.wait()

    @pl.when(s > 0)
    def _():
        ucat[2] = jnp.zeros((KB * BLK, R), BF16)

    @pl.when(s != 1)
    def _():
        pcs[nl + 2] = jnp.zeros((KB * BLK, R), BF16)

    pairs = []
    for d in (1, 2):
        read = lambda j, k, d=d: ms[d - 1, j, k]
        rd, rr = slots(read, s + d)
        for q in range(width[d]):
            entry = []
            for k in range(KB):
                t = jnp.int32(-1)
                for j in range(nl):
                    t = jnp.where((rd[j] == d) & (rr[j] == q), read(j, k), t)
                entry.append(t)
            targets.append(entry)
            pairs.append((row_ids(entry), ucat, first[d] + q))
    third = pairs.pop(2)

    def put_more(rows, total):
        accm[rows, :] += total

    @pl.when(s == 0)
    def _():
        updates(1, True).wait_recv()
        scatter(0, SA // 256, [third], put_more)

    even = lax.rem(s, 2) == 0
    near, far = pairs[:2], pairs[2:]

    def arrived(d):
        pl.when(s + d < S)(lambda: updates(d, False).wait_recv())

    @pl.when(even)
    def _():
        arrived(1)
        scatter(0, SA // 256, near, put_more)
        arrived(2)

    @pl.when(jnp.logical_not(even))
    def _():
        arrived(2)
        scatter(0, SA // 256, far, put_more)
        arrived(1)
    pairs = [
        (jnp.where(even, q[0], p[0]), ucat, jnp.where(even, q[2], p[2])) for p, q in zip(near, far)
    ]

    def pair(o, b):
        return remote(accs.at[o, b], pr.at[o, b], p_ss.at[o, b], p_rs.at[o, b], partner)

    def across(to, frm, b):
        return remote(ysnd.at[to, b], yrcv.at[frm, b], y_ss.at[to, b], y_rs.at[frm, b], (s, to * 2 + c))

    def rows_at(o, core, b):
        return pl.ds(pl.multiple_of((o * 2 + core) * SH + b * WSN, WSN), WSN)

    def more(o, core, b):
        scatter((o * 2 + core) * SH + b * WSN, WSN // 256, pairs, put_more)

    order = [lax.rem(y + i, ny) for i in range(1, ny)] + [y]
    for o in order:
        for b in range(B):
            more(o, 1 - c, b)
            accs[o, b] = accm[rows_at(o, 1 - c, b), :].astype(BF16)
            pair(o, b).start()
            more(o, c, b)
            if o is not y:
                pair(o, b).wait_recv()
                ysnd[o, b] = (accm[rows_at(o, c, b), :] + pr[o, b].astype(F32)).astype(BF16)
                across(o, y, b).start()
    big[0].wait()
    big[1].wait()
    big[2].wait()

    def right_side(b):
        at = pl.ds(b * WSN, WSN)
        pair(y, b).wait_recv()
        side = srt[at, :].astype(F32) - accm[rows_at(y, c, b), :] - pr[y, b].astype(F32)
        for o in order[:-1]:
            across(o, o, b).wait_recv()
            side = side - yrcv[o, b].astype(F32)
        run[at, :] = side.astype(BF16).astype(F32)

    def cols(q):
        return pl.ds(pl.multiple_of(q * WSN, WSN), WSN)

    def forward(q):
        return remote(yb.at[q], yb.at[q], f_ss.at[q], f_rs.at[q], up)

    @pl.when(m > 0)
    def _():
        for b in range(B):
            right_side(b)

    @pl.loop(0, m * B)
    def _(q):
        forward(q).wait_recv()
        pl.when(m < M - 1)(lambda: forward(q).start())
        for b in range(B):
            at = pl.ds(b * WSN, WSN)
            run[at, :] -= mm(fac[at, cols(q)], yb[q])

    for b in range(B):
        at = pl.ds(b * WSN, WSN)
        pl.when(m == 0)(lambda b=b: right_side(b))
        bracket = run[at, :]
        for e in range(b):
            bracket = bracket - mm(fac[at, cols(m * B + e)], yb[m * B + e])
        yb[m * B + b] = mm(sinv[at, :], bracket.astype(BF16)).astype(BF16)
        pl.when(m < M - 1)(lambda b=b: forward(m * B + b).start())
    for b in range(B):
        runt[:, b * WSN:(b + 1) * WSN] = yb[m * B + b].astype(F32).T

    def back(q):
        return remote(tsnd.at[q], trcv.at[q], t_ss.at[q], t_rs.at[q], down)

    nbs = WSN // BLK

    def xdown(q):
        part = xb.at[pl.ds(q * nbs, nbs)]
        return remote(part, part, xd_ss.at[q], xd_rs.at[q], down)

    def xup(q, to):
        part = xb.at[pl.ds(q * nbs, nbs)]
        return remote(part, part, xu_ss.at[q, to], xu_rs.at[q], (s, to))

    def later_chips(act):
        for o in range(1, ny):
            pl.when(o > y)(lambda o=o: act(2 * o))

    def turn_x(b):
        block = xt[:, b * WSN:(b + 1) * WSN].astype(F32).T.astype(BF16)
        q = m * B + b
        xb[pl.ds(q * nbs, nbs)] = block.reshape(nbs, BLK, R)

    def send_x(b):
        q = m * B + b
        later_chips(lambda to: xup(q, to).start())
        pl.when(c == 0)(lambda: xup(q, m + 1).start())
        pl.when(m > 0)(lambda: xdown(q).start())

    for b in reversed(range(B)):
        at = pl.ds(b * WSN, WSN)

        @pl.when(m < M - 1)
        def _():
            back(m * B + b).wait_recv()
            runt[:, at] -= trcv[m * B + b].astype(F32)
        bracket = runt[:, at]
        for e in range(b + 1, B):
            rows = pl.ds(e * WSN, WSN)
            bracket = bracket - mm(xt[:, rows], fac[rows, cols(m * B + b)])
        xt[:, at] = mm(bracket.astype(BF16), sinv[at, :]).astype(BF16)

        @pl.when(m == 0)
        def _():
            turn_x(b)
            send_x(b)

    @pl.loop(0, m * B)
    def _(i):
        q = m * B - 1 - i
        pl.when(m < M - 1)(lambda: back(q).wait_recv())
        term = mm(xt[...], fac[:, cols(q)])
        before = jnp.where(m < M - 1, trcv[q].astype(F32), 0.0)
        tsnd[q] = (term + before).astype(BF16)
        back(q).start()

    @pl.when(m > 0)
    def _():
        for b in reversed(range(B)):
            turn_x(b)

        @pl.loop(0, m * B)
        def _(q):
            back(q).wait_send()
        for b in reversed(range(B)):
            send_x(b)

    out_sep = pltpu.make_async_copy(xb.at[pl.ds(m * nbm, nbm)], osx, osem.at[nl])
    out_sep.start()

    @pl.loop(0, (M - 1 - m) * B)
    def _(i):
        q = M * B - 1 - i
        xdown(q).wait_recv()
        pl.when(m > 0)(lambda: xdown(q).start())

    @pl.loop(0, m * B)
    def _(i):
        q = m * B - 1 - i
        xup(q, m).wait_recv()
        pl.when(c == 0)(lambda: xup(q, m + 1).start())

    def pieces(d, third):
        if third:
            return remote(psnd.at[2], pcs.at[nl + 2], b_ss.at[2], b_rs.at[2], (s + d, m))
        a = psnd.at[pl.ds(first[d], 2)]
        b = pcs.at[pl.ds(base[d], 2)]
        return remote(a, b, b_ss.at[d - 1], b_rs.at[d - 1], (s + d, m))

    for d in (2, 1):
        @pl.when(s + d < S)
        def _():
            for q in range(width[d]):
                for k in range(KB):
                    t = jnp.maximum(targets[base[d] + q][k], 0)
                    psnd[first[d] + q, k * BLK:(k + 1) * BLK, :] = xb[t]
            pieces(d, False).start()
    pl.when(s == 0)(lambda: pieces(1, True).start())
    for j in range(nl):
        for k in range(KB):
            pcs[j, k * BLK:(k + 1) * BLK, :] = xb[block_s[j, k]]
    for d in (1, 2):
        pl.when(s >= d)(lambda d=d: pieces(d, False).wait_recv())
    pl.when(s == 1)(lambda: pieces(1, True).wait_recv())

    for j in range(nl):
        at = jnp.where(dist[j] == 0, j, jnp.where(dist[j] == 1, nl + rank[j], nl + c1 + rank[j]))
        at = jnp.clip(at, 0, nslots - 1)
        reduced = mm(pnt[j], pcs[at])
        inner = (ly[j].astype(F32) - reduced).astype(BF16)
        lo[j] = mm(ivt[j], inner).astype(BF16)
        pltpu.make_async_copy(lo.at[j], ox.at[j], osem.at[j]).start()

    for d in (1, 2):
        @pl.when(s >= d)
        def _():
            metas(d).wait_send()
            updates(d, False).wait_send()

        pl.when(s + d < S)(lambda d=d: pieces(d, False).wait_send())
    pl.when(s == 1)(lambda: updates(1, True).wait_send())
    pl.when(s == 0)(lambda: pieces(1, True).wait_send())
    for o in order:
        for b in range(B):
            pair(o, b).wait_send()
            if o is not y:
                across(o, y, b).wait_send()

    @pl.when(m < M - 1)
    def _():
        @pl.loop(0, (m + 1) * B)
        def _(q):
            forward(q).wait_send()

    @pl.when(c == 0)
    def _():
        @pl.loop(0, (m + 1) * B)
        def _(q):
            xup(q, m + 1).wait_send()

    for b in range(B):
        later_chips(lambda to, b=b: xup(m * B + b, to).wait_send())

    @pl.when(m > 0)
    def _():
        @pl.loop(m * B, M * B)
        def _(q):
            xdown(q).wait_send()

    out_sep.wait()
    for j in range(nl):
        pltpu.make_async_copy(lo.at[j], ox.at[j], osem.at[j]).wait()


def write_out(leaf_v, sep_v, ox, osx, sem):
    nl = leaf_v.shape[0]
    half = sep_v.shape[0] // 2
    copies = [pltpu.make_async_copy(leaf_v.at[j], ox.at[j], sem.at[j]) for j in range(nl)]
    for i in range(2):
        part = pl.ds(i * half, half)
        copies.append(pltpu.make_async_copy(sep_v.at[part], osx.at[part], sem.at[nl + i]))
    for copy in copies:
        copy.start()
    for copy in copies:
        copy.wait()


def shards(S, M, leaf_right, leaf_inverse, panels, leaf_subtree, panel_block, separator_right, separator_inverse, separator_factor):
    nl, W = leaf_right.shape[:2]
    SH = separator_right.shape[0]
    ny = M // 2
    nbm = SH // BLK
    B = SH // WSN
    N = SA // WSN
    nslots = 3 * nl - 3
    anywhere = pl.BlockSpec(memory_space=pl.ANY)
    V = pltpu.VMEM
    D = pltpu.SemaphoreType.DMA
    scratch = [
        V((nl, W, R), BF16), V((nl, W, W), BF16), V((nl, KB * BLK, W), BF16),
        V((SH, R), BF16), V((SH, WSN), BF16), V((SH, SA), BF16),
        V((nl, W, W), BF16), V((nl, W, KB * BLK), BF16),
        V((nl, W, R), BF16), V((nl, KB * BLK, R), BF16), V((2 * nl - 3, KB * BLK, R), BF16), V((2 * nl - 3, KB * BLK, R), BF16),
        V((8, 128), jnp.int32), V((2, 8, 128), jnp.int32), pltpu.SMEM((2, 8, 128), jnp.int32),
        V((SA, R), F32), V((ny, B, WSN, R), BF16), V((ny, B, WSN, R), BF16), V((ny, B, WSN, R), BF16), V((ny, B, WSN, R), BF16),
        V((SH, R), F32), V((N, WSN, R), BF16), V((R, SH), F32), V((R, SH), BF16),
        V((N, R, WSN), BF16), V((N, R, WSN), BF16), V((SA // BLK, BLK, R), BF16),
        V((nslots, KB * BLK, R), BF16), V((2 * nl - 3, KB * BLK, R), BF16), V((nl, W, R), BF16),
        D((3 * nl + 3,)), D((2,)), D((nl + 1,)),
        D((3,)), D((3,)), D((2,)), D((2,)), D((ny, B)), D((ny, B)), D((ny, B)), D((ny, B)),
        D((N,)), D((N,)), D((N,)), D((N,)), D((N,)), D((N,)), D((N, M)), D((N,)), D((3,)), D((3,)),
    ]
    leaf_x, sep_x = pl.pallas_call(
        functools.partial(kernel, S, M),
        out_shape=(
            jax.ShapeDtypeStruct((nl, W, R), BF16),
            jax.ShapeDtypeStruct((nbm, BLK, R), BF16),
        ),
        in_specs=[
            anywhere, anywhere, anywhere,
            pl.BlockSpec(memory_space=pltpu.SMEM), pl.BlockSpec(memory_space=pltpu.SMEM),
            anywhere, anywhere, anywhere,
        ],
        out_specs=(anywhere, anywhere),
        scratch_shapes=scratch,
        compiler_params=pltpu.CompilerParams(
            collective_id=0, has_side_effects=True, vmem_limit_bytes=56 * 1024 * 1024
        ),
        cost_estimate=pl.CostEstimate(flops=12_000_000_000, bytes_accessed=16_000_000, transcendentals=0),
    )(leaf_right, leaf_inverse, panels, panel_block, leaf_subtree, separator_right, separator_inverse, separator_factor)
    leaf_x, sep_x = pl.pallas_call(
        write_out,
        out_shape=(
            jax.ShapeDtypeStruct((nl, W, R), BF16),
            jax.ShapeDtypeStruct((nbm, BLK, R), BF16),
        ),
        in_specs=[pl.BlockSpec(memory_space=pltpu.VMEM)] * 2,
        out_specs=(anywhere, anywhere),
        scratch_shapes=[D((nl + 2,))],
        cost_estimate=pl.CostEstimate(flops=0, bytes_accessed=3_000_000, transcendentals=0),
    )(leaf_x, sep_x)
    return leaf_x, sep_x.reshape(SH, R)


def solution(mesh):
    placed = (
        P(("leaf", "sub"), None, None),
        P(("leaf", "sub"), None, None),
        P(("leaf", "sub"), None, None),
        P(("leaf", "sub")),
        P(("leaf", "sub"), None),
        P(("leaf", "sub"), None),
        P(("leaf", "sub"), None),
        P(("leaf", "sub"), None),
    )
    return jax.shard_map(
        functools.partial(shards, mesh.shape["leaf"], mesh.shape["sub"]),
        mesh=mesh,
        in_specs=placed,
        out_specs=(P(("leaf", "sub"), None, None), P(("leaf", "sub"), None)),
        check_vma=False,
    )
```

```python
import functools

import jax
import jax.numpy as jnp
from jax import lax
from jax.experimental import pallas as pl
from jax.experimental.pallas import tpu as pltpu
from jax.sharding import PartitionSpec as P

WSN = 512
SA = 4096
R = 256
BLK = 64
KB = 4
SPAN = 3
MESH = pl.DeviceIdType.MESH
F32 = jnp.float32
BF16 = jnp.bfloat16


def mm(a, b):
    return jnp.dot(a, b, preferred_element_type=F32)


def mm_t(a, b):
    return lax.dot_general(a, b, (((0,), (0,)), ((), ())), preferred_element_type=F32)


def kernel(
    S, M,
    right_h, inv_h, panels_h, block_s, tree_s, sright_h, sinv_h, fac_h,
    ox, osx,
    rt, iv, pn, srt, sinv, fac,
    ivt, pnt, ly, ub, ucat, usnd, mv, mr, ms,
    accm, accs, pr, ysnd, yrcv, run, yb, runt, xt, trcv, tsnd, xb, pcs, psnd, lo,
    lsem, msem, osem,
    u_ss, u_rs, m_ss, m_rs, p_ss, p_rs, y_ss, y_rs, f_ss, f_rs, t_ss, t_rs,
    xd_ss, xd_rs, xu_ss, xu_rs, b_ss, b_rs,
):
    s = lax.axis_index("leaf")
    m = lax.axis_index("sub")
    c = lax.rem(m, 2)
    y = lax.div(m, 2)
    ny = M // 2
    nl = right_h.shape[0]
    SH = srt.shape[0]
    B = SH // WSN
    nbm = SH // BLK
    c1, c2 = nl - 1, nl - 2
    first = {1: 0, 2: c1}
    base = {1: nl, 2: nl + c1}
    width = {1: c1, 2: c2}
    nslots = nl + c1 + c2
    partner = (s, m + 1 - 2 * c)
    up = (s, m + 1)
    down = (s, m - 1)

    def remote(src, dst, ssem, rsem, dev):
        return pltpu.make_async_remote_copy(
            src_ref=src, dst_ref=dst, send_sem=ssem, recv_sem=rsem, device_id=dev, device_id_type=MESH
        )

    locals_in = [
        (right_h, rt, 0), (inv_h, iv, nl), (panels_h, pn, 2 * nl),
    ]
    for j in range(nl):
        for src, dst, at in locals_in:
            pltpu.make_async_copy(src.at[j], dst.at[j], lsem.at[at + j]).start()
    big = [
        pltpu.make_async_copy(sright_h, srt, lsem.at[3 * nl]),
        pltpu.make_async_copy(sinv_h, sinv, lsem.at[3 * nl + 1]),
        pltpu.make_async_copy(fac_h, fac, lsem.at[3 * nl + 2]),
    ]
    for copy in big:
        copy.start()

    barrier = pltpu.get_barrier_semaphore()

    def greet(dev):
        pl.semaphore_signal(barrier, inc=1, device_id=dev, device_id_type=MESH)

    def when_greet(cond, dev):
        pl.when(cond)(lambda: greet(dev))
        return cond.astype(jnp.int32)

    friends = jnp.int32(M - 1)
    for i in range(1, M):
        greet((s, lax.rem(m + i, M)))
    for d in (1, 2):
        friends = friends + when_greet(s >= d, (s - d, m))
        friends = friends + when_greet(s + d < S, (s + d, m))

    @pl.loop(0, nl)
    def _(j):
        for src, dst, at in locals_in:
            pltpu.make_async_copy(src.at[j], dst.at[j], lsem.at[at + j]).wait()
        sol = mm(iv[j], rt[j]).astype(BF16)
        ly[j] = sol
        ub[j] = mm(pn[j], sol).astype(BF16)

    def slots(read, sec):
        dist = [sec - read(j, KB) for j in range(nl)]
        rank = []
        for j in range(nl):
            r = jnp.int32(0)
            for i in range(j):
                r = r + (dist[i] == dist[j]).astype(jnp.int32)
            rank.append(r)
        return dist, rank

    own = lambda j, k: tree_s[j] if k == KB else block_s[j, k]
    sub = lax.broadcasted_iota(jnp.int32, mv.shape, 0)
    lane = lax.broadcasted_iota(jnp.int32, mv.shape, 1)
    meta = jnp.zeros(mv.shape, jnp.int32)
    for j in range(nl):
        for k in range(KB + 1):
            meta = jnp.where((sub == j) & (lane == k), own(j, k), meta)
    mv[...] = meta
    dist, rank = slots(own, s)

    pl.semaphore_wait(barrier, friends)

    def metas(d):
        return remote(mv, mr.at[d - 1], m_ss.at[d - 1], m_rs.at[d - 1], (s - d, m))

    def updates(d, third):
        if third:
            a, b = usnd.at[2], ucat.at[2]
            return remote(a, b, u_ss.at[2], u_rs.at[2], (s - d, m))
        a = usnd.at[pl.ds(first[d], 2)]
        b = ucat.at[pl.ds(first[d], 2)]
        return remote(a, b, u_ss.at[d - 1], u_rs.at[d - 1], (s - d, m))

    for d in (2, 1):
        @pl.when(s >= d)
        def _():
            metas(d).start()
            for q in range(width[d]):
                pick = jnp.int32(0)
                for j in range(nl):
                    pick = jnp.where((dist[j] == d) & (rank[j] == q), j, pick)
                usnd[first[d] + q] = ub[pick]
            updates(d, False).start()
    pl.when(s == 1)(lambda: updates(1, True).start())

    def row_ids(entry):
        lane = lax.broadcasted_iota(jnp.int32, (1, KB * BLK), 1)
        v = jnp.full((1, KB * BLK), entry[KB - 1] * BLK, jnp.int32)
        for k in range(KB - 1):
            v = jnp.where(lane // BLK == k, entry[k] * BLK, v)
        return v + lane % BLK

    def scatter(begin, blocks, pairs, put):
        @pl.loop(0, blocks)
        def _(i):
            at = begin + i * 256
            iota = lax.broadcasted_iota(jnp.int32, (256, KB * BLK), 0) + at
            total = jnp.zeros((256, R), F32)
            for ids, ref, n in pairs:
                pick = jnp.where(iota == ids, 1.0, 0.0).astype(BF16)
                total = total + mm(pick, ref[n])
            put(pl.ds(pl.multiple_of(at, 256), 256), total)

    targets = []
    for j in range(nl):
        targets.append([jnp.where(dist[j] == 0, block_s[j, k], -1) for k in range(KB)])
    pairs = [(row_ids(targets[j]), ub, j) for j in range(nl)]

    def put_own(rows, total):
        accm[rows, :] = total
    scatter(0, SA // 256, pairs, put_own)

    @pl.loop(0, nl)
    def _(j):
        ivt[j] = iv[j].astype(F32).T.astype(BF16)
        pnt[j] = pn[j].astype(F32).T.astype(BF16)

    for d in (1, 2):
        @pl.when(s + d < S)
        def _():
            metas(d).wait_recv()

        @pl.when(s + d >= S)
        def _():
            mr[d - 1] = jnp.full(mr.shape[1:], -1000, jnp.int32)
            ucat[first[d]:first[d] + 2] = jnp.zeros((2, KB * BLK, R), BF16)

        @pl.when(s < d)
        def _():
            pcs[base[d]:base[d] + 2] = jnp.zeros((2, KB * BLK, R), BF16)
        copy = pltpu.make_async_copy(mr.at[d - 1], ms.at[d - 1], msem.at[d - 1])
        copy.start()
        copy.wait()

    @pl.when(s > 0)
    def _():
        ucat[2] = jnp.zeros((KB * BLK, R), BF16)

    @pl.when(s != 1)
    def _():
        pcs[nl + 2] = jnp.zeros((KB * BLK, R), BF16)

    pairs = []
    for d in (1, 2):
        read = lambda j, k, d=d: ms[d - 1, j, k]
        rd, rr = slots(read, s + d)
        for q in range(width[d]):
            entry = []
            for k in range(KB):
                t = jnp.int32(-1)
                for j in range(nl):
                    t = jnp.where((rd[j] == d) & (rr[j] == q), read(j, k), t)
                entry.append(t)
            targets.append(entry)
            pairs.append((row_ids(entry), ucat, first[d] + q))
    third = pairs.pop(2)

    def put_more(rows, total):
        accm[rows, :] += total

    @pl.when(s == 0)
    def _():
        updates(1, True).wait_recv()
        scatter(0, SA // 256, [third], put_more)

    even = lax.rem(s, 2) == 0
    near, far = pairs[:2], pairs[2:]

    def arrived(d):
        pl.when(s + d < S)(lambda: updates(d, False).wait_recv())

    @pl.when(even)
    def _():
        arrived(1)
        scatter(0, SA // 256, near, put_more)
        arrived(2)

    @pl.when(jnp.logical_not(even))
    def _():
        arrived(2)
        scatter(0, SA // 256, far, put_more)
        arrived(1)
    pairs = [
        (jnp.where(even, q[0], p[0]), ucat, jnp.where(even, q[2], p[2])) for p, q in zip(near, far)
    ]

    def pair(o, b):
        return remote(accs.at[o, b], pr.at[o, b], p_ss.at[o, b], p_rs.at[o, b], partner)

    def across(to, frm, b):
        return remote(ysnd.at[to, b], yrcv.at[frm, b], y_ss.at[to, b], y_rs.at[frm, b], (s, to * 2 + c))

    def rows_at(o, core, b):
        return pl.ds(pl.multiple_of((o * 2 + core) * SH + b * WSN, WSN), WSN)

    def more(o, core, b):
        scatter((o * 2 + core) * SH + b * WSN, WSN // 256, pairs, put_more)

    order = [lax.rem(y + i, ny) for i in range(1, ny)] + [y]
    for o in order:
        for b in range(B):
            more(o, 1 - c, b)
            accs[o, b] = accm[rows_at(o, 1 - c, b), :].astype(BF16)
            pair(o, b).start()
            more(o, c, b)
            if o is not y:
                pair(o, b).wait_recv()
                ysnd[o, b] = (accm[rows_at(o, c, b), :] + pr[o, b].astype(F32)).astype(BF16)
                across(o, y, b).start()
    big[0].wait()
    big[1].wait()
    big[2].wait()

    def right_side(b):
        at = pl.ds(b * WSN, WSN)
        pair(y, b).wait_recv()
        side = srt[at, :].astype(F32) - accm[rows_at(y, c, b), :] - pr[y, b].astype(F32)
        for o in order[:-1]:
            across(o, o, b).wait_recv()
            side = side - yrcv[o, b].astype(F32)
        run[at, :] = side.astype(BF16).astype(F32)

    def cols(q):
        return pl.ds(pl.multiple_of(q * WSN, WSN), WSN)

    def forward(q):
        return remote(yb.at[q], yb.at[q], f_ss.at[q], f_rs.at[q], up)

    @pl.when(m > 0)
    def _():
        for b in range(B):
            right_side(b)

    @pl.loop(0, m * B)
    def _(q):
        forward(q).wait_recv()
        pl.when(m < M - 1)(lambda: forward(q).start())
        for b in range(B):
            at = pl.ds(b * WSN, WSN)
            run[at, :] -= mm(fac[at, cols(q)], yb[q])

    for b in range(B):
        at = pl.ds(b * WSN, WSN)
        pl.when(m == 0)(lambda b=b: right_side(b))
        bracket = run[at, :]
        for e in range(b):
            bracket = bracket - mm(fac[at, cols(m * B + e)], yb[m * B + e])
        yb[m * B + b] = mm(sinv[at, :], bracket.astype(BF16)).astype(BF16)
        pl.when(m < M - 1)(lambda b=b: forward(m * B + b).start())
    for b in range(B):
        runt[:, b * WSN:(b + 1) * WSN] = yb[m * B + b].astype(F32).T

    def back(q):
        return remote(tsnd.at[q], trcv.at[q], t_ss.at[q], t_rs.at[q], down)

    nbs = WSN // BLK

    def xdown(q):
        part = xb.at[pl.ds(q * nbs, nbs)]
        return remote(part, part, xd_ss.at[q], xd_rs.at[q], down)

    def xup(q, to):
        part = xb.at[pl.ds(q * nbs, nbs)]
        return remote(part, part, xu_ss.at[q, to], xu_rs.at[q], (s, to))

    def later_chips(act):
        for o in range(1, ny):
            pl.when(o > y)(lambda o=o: (act(2 * o + 1), act(2 * o)) and None)

    def turn_x(b):
        block = xt[:, b * WSN:(b + 1) * WSN].astype(F32).T.astype(BF16)
        q = m * B + b
        xb[pl.ds(q * nbs, nbs)] = block.reshape(nbs, BLK, R)

    def send_x(b):
        q = m * B + b
        later_chips(lambda to: xup(q, to).start())
        pl.when(c == 0)(lambda: xup(q, m + 1).start())
        pl.when(m > 0)(lambda: xdown(q).start())

    for b in reversed(range(B)):
        at = pl.ds(b * WSN, WSN)

        @pl.when(m < M - 1)
        def _():
            back(m * B + b).wait_recv()
            runt[:, at] -= trcv[m * B + b].astype(F32)
        bracket = runt[:, at]
        for e in range(b + 1, B):
            rows = pl.ds(e * WSN, WSN)
            bracket = bracket - mm(xt[:, rows], fac[rows, cols(m * B + b)])
        xt[:, at] = mm(bracket.astype(BF16), sinv[at, :]).astype(BF16)

        @pl.when(m == 0)
        def _():
            turn_x(b)
            send_x(b)

    @pl.loop(0, m * B)
    def _(i):
        q = m * B - 1 - i
        pl.when(m < M - 1)(lambda: back(q).wait_recv())
        term = mm(xt[...], fac[:, cols(q)])
        before = jnp.where(m < M - 1, trcv[q].astype(F32), 0.0)
        tsnd[q] = (term + before).astype(BF16)
        back(q).start()

    @pl.when(m > 0)
    def _():
        for b in reversed(range(B)):
            turn_x(b)

        @pl.loop(0, m * B)
        def _(q):
            back(q).wait_send()
        for b in reversed(range(B)):
            send_x(b)

    out_sep = pltpu.make_async_copy(xb.at[pl.ds(m * nbm, nbm)], osx, osem.at[nl])
    out_sep.start()

    @pl.loop(0, (M - 1 - m) * B)
    def _(i):
        q = M * B - 1 - i
        xdown(q).wait_recv()
        pl.when(m > 0)(lambda: xdown(q).start())

    @pl.loop(0, m * B)
    def _(i):
        q = m * B - 1 - i
        xup(q, m).wait_recv()

    def pieces(d, third):
        if third:
            return remote(psnd.at[2], pcs.at[nl + 2], b_ss.at[2], b_rs.at[2], (s + d, m))
        a = psnd.at[pl.ds(first[d], 2)]
        b = pcs.at[pl.ds(base[d], 2)]
        return remote(a, b, b_ss.at[d - 1], b_rs.at[d - 1], (s + d, m))

    for d in (2, 1):
        @pl.when(s + d < S)
        def _():
            for q in range(width[d]):
                for k in range(KB):
                    t = jnp.maximum(targets[base[d] + q][k], 0)
                    psnd[first[d] + q, k * BLK:(k + 1) * BLK, :] = xb[t]
            pieces(d, False).start()
    pl.when(s == 0)(lambda: pieces(1, True).start())
    for j in range(nl):
        for k in range(KB):
            pcs[j, k * BLK:(k + 1) * BLK, :] = xb[block_s[j, k]]
    for d in (1, 2):
        pl.when(s >= d)(lambda d=d: pieces(d, False).wait_recv())
    pl.when(s == 1)(lambda: pieces(1, True).wait_recv())

    for j in range(nl):
        at = jnp.where(dist[j] == 0, j, jnp.where(dist[j] == 1, nl + rank[j], nl + c1 + rank[j]))
        at = jnp.clip(at, 0, nslots - 1)
        reduced = mm(pnt[j], pcs[at])
        inner = (ly[j].astype(F32) - reduced).astype(BF16)
        lo[j] = mm(ivt[j], inner).astype(BF16)
        pltpu.make_async_copy(lo.at[j], ox.at[j], osem.at[j]).start()

    for d in (1, 2):
        @pl.when(s >= d)
        def _():
            metas(d).wait_send()
            updates(d, False).wait_send()

        pl.when(s + d < S)(lambda d=d: pieces(d, False).wait_send())
    pl.when(s == 1)(lambda: updates(1, True).wait_send())
    pl.when(s == 0)(lambda: pieces(1, True).wait_send())
    for o in order:
        for b in range(B):
            pair(o, b).wait_send()
            if o is not y:
                across(o, y, b).wait_send()

    @pl.when(m < M - 1)
    def _():
        @pl.loop(0, (m + 1) * B)
        def _(q):
            forward(q).wait_send()

    @pl.when(c == 0)
    def _():
        @pl.loop(m * B, (m + 1) * B)
        def _(q):
            xup(q, m + 1).wait_send()

    for b in range(B):
        later_chips(lambda to, b=b: xup(m * B + b, to).wait_send())

    @pl.when(m > 0)
    def _():
        @pl.loop(m * B, M * B)
        def _(q):
            xdown(q).wait_send()

    out_sep.wait()
    for j in range(nl):
        pltpu.make_async_copy(lo.at[j], ox.at[j], osem.at[j]).wait()


def write_out(leaf_v, sep_v, ox, osx, sem):
    nl = leaf_v.shape[0]
    half = sep_v.shape[0] // 2
    copies = [pltpu.make_async_copy(leaf_v.at[j], ox.at[j], sem.at[j]) for j in range(nl)]
    for i in range(2):
        part = pl.ds(i * half, half)
        copies.append(pltpu.make_async_copy(sep_v.at[part], osx.at[part], sem.at[nl + i]))
    for copy in copies:
        copy.start()
    for copy in copies:
        copy.wait()


def shards(S, M, leaf_right, leaf_inverse, panels, leaf_subtree, panel_block, separator_right, separator_inverse, separator_factor):
    nl, W = leaf_right.shape[:2]
    SH = separator_right.shape[0]
    ny = M // 2
    nbm = SH // BLK
    B = SH // WSN
    N = SA // WSN
    nslots = 3 * nl - 3
    anywhere = pl.BlockSpec(memory_space=pl.ANY)
    V = pltpu.VMEM
    D = pltpu.SemaphoreType.DMA
    scratch = [
        V((nl, W, R), BF16), V((nl, W, W), BF16), V((nl, KB * BLK, W), BF16),
        V((SH, R), BF16), V((SH, WSN), BF16), V((SH, SA), BF16),
        V((nl, W, W), BF16), V((nl, W, KB * BLK), BF16),
        V((nl, W, R), BF16), V((nl, KB * BLK, R), BF16), V((2 * nl - 3, KB * BLK, R), BF16), V((2 * nl - 3, KB * BLK, R), BF16),
        V((8, 128), jnp.int32), V((2, 8, 128), jnp.int32), pltpu.SMEM((2, 8, 128), jnp.int32),
        V((SA, R), F32), V((ny, B, WSN, R), BF16), V((ny, B, WSN, R), BF16), V((ny, B, WSN, R), BF16), V((ny, B, WSN, R), BF16),
        V((SH, R), F32), V((N, WSN, R), BF16), V((R, SH), F32), V((R, SH), BF16),
        V((N, R, WSN), BF16), V((N, R, WSN), BF16), V((SA // BLK, BLK, R), BF16),
        V((nslots, KB * BLK, R), BF16), V((2 * nl - 3, KB * BLK, R), BF16), V((nl, W, R), BF16),
        D((3 * nl + 3,)), D((2,)), D((nl + 1,)),
        D((3,)), D((3,)), D((2,)), D((2,)), D((ny, B)), D((ny, B)), D((ny, B)), D((ny, B)),
        D((N,)), D((N,)), D((N,)), D((N,)), D((N,)), D((N,)), D((N, M)), D((N,)), D((3,)), D((3,)),
    ]
    leaf_x, sep_x = pl.pallas_call(
        functools.partial(kernel, S, M),
        out_shape=(
            jax.ShapeDtypeStruct((nl, W, R), BF16),
            jax.ShapeDtypeStruct((nbm, BLK, R), BF16),
        ),
        in_specs=[
            anywhere, anywhere, anywhere,
            pl.BlockSpec(memory_space=pltpu.SMEM), pl.BlockSpec(memory_space=pltpu.SMEM),
            anywhere, anywhere, anywhere,
        ],
        out_specs=(anywhere, anywhere),
        scratch_shapes=scratch,
        compiler_params=pltpu.CompilerParams(
            collective_id=0, has_side_effects=True, vmem_limit_bytes=56 * 1024 * 1024
        ),
        cost_estimate=pl.CostEstimate(flops=12_000_000_000, bytes_accessed=16_000_000, transcendentals=0),
    )(leaf_right, leaf_inverse, panels, panel_block, leaf_subtree, separator_right, separator_inverse, separator_factor)
    leaf_x, sep_x = pl.pallas_call(
        write_out,
        out_shape=(
            jax.ShapeDtypeStruct((nl, W, R), BF16),
            jax.ShapeDtypeStruct((nbm, BLK, R), BF16),
        ),
        in_specs=[pl.BlockSpec(memory_space=pltpu.VMEM)] * 2,
        out_specs=(anywhere, anywhere),
        scratch_shapes=[D((nl + 2,))],
        cost_estimate=pl.CostEstimate(flops=0, bytes_accessed=3_000_000, transcendentals=0),
    )(leaf_x, sep_x)
    return leaf_x, sep_x.reshape(SH, R)


def solution(mesh):
    placed = (
        P(("leaf", "sub"), None, None),
        P(("leaf", "sub"), None, None),
        P(("leaf", "sub"), None, None),
        P(("leaf", "sub")),
        P(("leaf", "sub"), None),
        P(("leaf", "sub"), None),
        P(("leaf", "sub"), None),
        P(("leaf", "sub"), None),
    )
    return jax.shard_map(
        functools.partial(shards, mesh.shape["leaf"], mesh.shape["sub"]),
        mesh=mesh,
        in_specs=placed,
        out_specs=(P(("leaf", "sub"), None, None), P(("leaf", "sub"), None)),
        check_vma=False,
    )
```
